256 devices in a mesh: agent: 16 (over y, x), tensor: 16 (over z, core).
Axes of the slice: x: 4, y: 4, z: 8, core: 2. Of those that a mesh axis runs over, the one named last changes fastest.
Arguments:
- tokens: bfloat16 [8192, 4096], P('agent', 'tensor'), may hold values from -6 to 6
- valid: int32 [8192], P('agent'), may hold values from 0 to 1, as said below
- latents: bfloat16 [512, 4096], P(None, 'tensor'), may hold values from -6 to 6
- w_query: bfloat16 [4096, 4096], P('agent', 'tensor'), may hold values from -5.625 to 5.625
- w_key: bfloat16 [4096, 4096], P('agent', 'tensor'), may hold values from -0.09375 to 0.09375
- w_value: bfloat16 [4096, 4096], P('agent', 'tensor'), may hold values from -0.09375 to 0.09375
- w_out: bfloat16 [4096, 4096], P('agent', 'tensor'), may hold values from -0.09375 to 0.09375
- gain: float32 [4096], P('tensor'), may hold values from 0.25 to 1.75
Outputs:
- updated: bfloat16 [512, 4096], P(None, 'tensor')
- normed: bfloat16 [512, 4096], P(None, 'tensor')
The draws below stay inside these ranges and needn't reach their ends.
Inputs may be any that keep to these rules, and one draw needn't show every extreme that they name: Each block of 512 agents has its own share of valid agents, from an eighth to all.
All inputs are finite; a program needn't handle non-finite values.
Results may differ from the reference program's by a relative error of at most 0.0034.
The reference program's roundings to bfloat16 on the way (of `query` and `attended`) count: a program that leaves them out, or rounds other values in their place, can miss the bound.
Values may be sent and summed in bfloat16 or wider, within the bound.
No kernel may reach another device: no remote copies, remote signals or barrier semaphores. Data moves between devices by JAX's collectives and lax.ppermute only.
A program may use at most 64 MiB of HBM per device.

```python
import jax
import jax.numpy as jnp
from jax import lax

HEADS = 32
HEAD_DIM = 128
D = 4096
LATENTS = 512
AG_DEV = 512
AGENTS = 8192


def draw_valid(key, part):
    key = jax.random.fold_in(key, 7)
    key_share, key_slot = jax.random.split(key)
    shares = jax.random.randint(key_share, (AGENTS // AG_DEV,), 1, 9)
    slots = jax.random.randint(key_slot, (AGENTS,), 0, 8)
    block_of = jnp.arange(AGENTS) // AG_DEV
    return (slots < shares[block_of]).astype(jnp.int32)


def draw_w_query(key, part):
    key = jax.random.fold_in(key, 11)
    key_base = jax.random.fold_in(key, 0)
    base = jnp.clip(jax.random.normal(key_base, (D, D), jnp.float32), -6.0, 6.0) * jnp.float32(D ** (-0.5))
    return base.astype(jnp.bfloat16)


def level_of(stream_key, dims, cuts, least, top_value):
    def one(axis_at, parts):
        steps = jax.random.uniform(jax.random.fold_in(jax.random.fold_in(stream_key, 6), axis_at), (parts,), jnp.float32, least / len(cuts), top_value / len(cuts))
        return jnp.repeat(jnp.exp(steps), dims[axis_at] // parts).reshape((-1,) + (1,) * (len(dims) - axis_at - 1))

    level = one(*cuts[0])
    for cut in cuts[1:]:
        level = level * one(*cut)
    return level


def bell_draw(stream_key, extent, spread, most, cuts=(), dtype=jnp.bfloat16):
    array = jax.random.normal(stream_key, extent, jnp.float32) * spread
    if len(cuts) > 0:
        array = level_of(stream_key, extent, cuts, -0.22, 0.18) * array
    return jnp.clip(array, min=-most, max=most).astype(dtype)


def setup_inputs(seed: int = 0) -> dict:
    splits = jax.random.split(jax.random.key(seed), 9)
    return {
        "tokens": bell_draw(splits[0], (AGENTS, D), 1.0, 6.0, ((0, 16), (1, 16))),
        "valid": draw_valid(jax.random.fold_in(splits[8], 71), 0),
        "latents": bell_draw(splits[2], (LATENTS, D), 1.0, 6.0, ((1, 16),)),
        "w_query": draw_w_query(jax.random.fold_in(splits[8], 71), 0),
        "w_key": bell_draw(splits[4], (D, D), D ** -0.5, 0.09375, ((0, 16), (1, 16))),
        "w_value": bell_draw(splits[5], (D, D), D ** -0.5, 0.09375, ((0, 16), (1, 16))),
        "w_out": bell_draw(splits[6], (D, D), D ** -0.5, 0.09375, ((0, 16), (1, 16))),
        "gain": jnp.clip(1.0 + 0.15 * jax.random.normal(splits[7], (D,), jnp.float32), 0.25, 1.75),
    }


def reference(tokens, valid, latents, w_query, w_key, w_value, w_out, gain):
    query = jnp.dot(latents, w_query, preferred_element_type=jnp.float32).astype(jnp.bfloat16)
    keys = jnp.dot(tokens, w_key, preferred_element_type=jnp.float32).astype(jnp.bfloat16)
    values = jnp.dot(tokens, w_value, preferred_element_type=jnp.float32).astype(jnp.bfloat16)
    q_heads = query.reshape(LATENTS, HEADS, HEAD_DIM).transpose(1, 0, 2)
    k_heads = keys.reshape(AGENTS, HEADS, HEAD_DIM).transpose(1, 0, 2)
    v_heads = values.reshape(AGENTS, HEADS, HEAD_DIM).transpose(1, 0, 2)
    keep = valid > 0
    scale = 1.0 / HEAD_DIM ** 0.5

    def one_head(items):
        q_one, k_one, v_one = items
        scores = jnp.dot(q_one, k_one.T, preferred_element_type=jnp.float32) * scale
        scores = jnp.where(keep[None, :], scores, jnp.float32(-1000000000.0))
        top = lax.optimization_barrier(jnp.max(scores, axis=1, keepdims=True))
        expo = jnp.exp(scores - top)
        total = lax.optimization_barrier(jnp.sum(expo, axis=1, keepdims=True))
        summed = jnp.dot(expo, v_one.astype(jnp.float32), precision=lax.Precision.HIGHEST)
        return summed / total
    attended = lax.map(one_head, (q_heads, k_heads, v_heads))
    attended = attended.transpose(1, 0, 2).reshape(LATENTS, D).astype(jnp.bfloat16)
    upd = latents.astype(jnp.float32) + jnp.dot(attended, w_out, preferred_element_type=jnp.float32)
    mean_sq = lax.optimization_barrier(jnp.mean(upd * upd, axis=1, keepdims=True))
    normed = gain[None, :] * upd * lax.rsqrt(mean_sq + 1e-05)
    return (upd.astype(jnp.bfloat16), normed.astype(jnp.bfloat16))
```

```python
import jax
import jax.numpy as jnp
from jax import lax
from jax.experimental import pallas as pl
from jax.experimental.pallas import tpu as pltpu
from jax.sharding import PartitionSpec as P

HEAD_DIM = 128
SIDE = 4
GROUP = 16
STEPS = (0, -1, 1, 2)
BF16 = jnp.bfloat16
F32 = jnp.float32


def hop_x(array, by):
    pairs = [(a, a // SIDE * SIDE + (a + by) % SIDE) for a in range(GROUP)]
    return lax.ppermute(array, "agent", pairs)


def hop_y(array, by):
    pairs = [(a, (a + by * SIDE) % GROUP) for a in range(GROUP)]
    return lax.ppermute(array, "agent", pairs)


def ring(block, hop):
    half = block.shape[0] // 2
    low = hop(block, 1)
    high = hop(block, -1)
    far_top = hop(low[:half], 1)
    far_bottom = hop(high[half:], -1)
    return block, low, high, far_top, far_bottom


def gather_weights(first, second, hop_one, hop_two):
    pair = jnp.concatenate([first, second], axis=0)
    line = jnp.concatenate(ring(pair, hop_one), axis=0)
    return ring(line, hop_two)


def attend_kernel(block_ids, feats, qk0, qk1, qk2, qk3, qk4, vo0, vo1, vo2, vo3, vo4, valid,
                  out, x_all, qk_all, v_all, stat, x_sem, qk_sem, v_sem):
    rows = feats.shape[1] // 2
    depth = feats.shape[2]
    x_copies = []
    for slot in range(GROUP):
        copy = pltpu.make_async_copy(feats.at[block_ids[slot]], x_all.at[slot], x_sem.at[slot])
        x_copies.append(copy)
    qk_parts = ((qk0, 0, 4), (qk1, 4, 4), (qk2, 8, 4), (qk3, 12, 2), (qk4, 14, 2))
    vo_parts = ((vo0, 0, 4), (vo1, 4, 4), (vo2, 8, 4), (vo3, 12, 2), (vo4, 14, 2))
    qk_copies, v_copies = [], []
    for n, (ref, start, count) in enumerate(qk_parts):
        qk_copies.append(pltpu.make_async_copy(
            ref, qk_all.at[pl.ds(start, count)], qk_sem.at[n]))
    for n, (ref, start, count) in enumerate(vo_parts):
        v_copies.append(pltpu.make_async_copy(
            ref.at[:, 0], v_all.at[pl.ds(start, count)], v_sem.at[n]))
    for part in range(SIDE):
        for copy in x_copies[part * SIDE:(part + 1) * SIDE]:
            copy.start()
        if part < 3:
            qk_copies[part].start()
        else:
            qk_copies[3].start()
            qk_copies[4].start()
    for copy in v_copies:
        copy.start()

    def columns(first, top):
        return jnp.concatenate(
            [x_all[first + j, pl.ds(top, rows), :] for j in range(SIDE)], axis=1)

    query = keys = values = None
    for part in range(SIDE):
        for copy in x_copies[part * SIDE:(part + 1) * SIDE]:
            copy.wait()
        if part < 3:
            qk_copies[part].wait()
        else:
            qk_copies[3].wait()
            qk_copies[4].wait()
        w_q = qk_all[pl.ds(part * SIDE, SIDE), 0].reshape(SIDE * depth, -1)
        w_k = qk_all[pl.ds(part * SIDE, SIDE), 1].reshape(SIDE * depth, -1)
        more_q = jnp.dot(columns(part * SIDE, rows), w_q, preferred_element_type=F32)
        more_k = jnp.dot(columns(part * SIDE, 0), w_k, preferred_element_type=F32)
        query = more_q if query is None else query + more_q
        keys = more_k if keys is None else keys + more_k
    for copy in v_copies:
        copy.wait()
    for part in range(SIDE):
        w_v = jnp.concatenate([v_all[j * SIDE + part] for j in range(SIDE)], axis=0)
        more_v = jnp.dot(columns(part * SIDE, 0), w_v, preferred_element_type=F32)
        values = more_v if values is None else values + more_v
    query = query.astype(BF16)
    keys = keys.astype(BF16)
    values = values.astype(BF16)
    scale = 1.0 / HEAD_DIM**0.5
    keep = valid[...] > 0
    lane = lax.broadcasted_iota(jnp.int32, (rows, HEAD_DIM), 1)
    tile = lax.broadcasted_iota(jnp.int32, (rows, HEAD_DIM), 0) // 8 % 4
    packed = jnp.zeros((rows, HEAD_DIM), F32)
    chunk = rows // GROUP
    for head in range(2):
        cols = slice(head * HEAD_DIM, (head + 1) * HEAD_DIM)
        scores = lax.dot_general(query[:, cols], keys[:, cols], (((1,), (1,)), ((), ())),
                                 preferred_element_type=F32) * scale
        scores = jnp.where(keep, scores, jnp.float32(-1000000000.0))
        top = jnp.max(scores, axis=1, keepdims=True)
        expo = jnp.exp(scores - top)
        total = jnp.sum(expo, axis=1, keepdims=True)
        coarse = expo.astype(BF16)
        fine = (expo - coarse.astype(F32)).astype(BF16)
        summed = jnp.dot(coarse, values[:, cols], preferred_element_type=F32)
        summed += jnp.dot(fine, values[:, cols], preferred_element_type=F32)
        out[:, pl.ds(head * chunk, chunk), :] = summed.reshape(GROUP, chunk, HEAD_DIM)
        packed = jnp.where(lane == 4 * tile + 2 * head, top, packed)
        packed = jnp.where(lane == 4 * tile + 2 * head + 1, total, packed)
    stat[...] = packed.reshape(GROUP, chunk // 8, 8, HEAD_DIM)
    out[:, pl.ds(2 * chunk, 8), :] = stat[:, 0] + stat[:, 1] + stat[:, 2] + stat[:, 3]


def combine_kernel(parts, out):
    chunk = out.shape[1]
    for tile in range(chunk // 8):
        for head in range(2):
            at = 4 * tile + 2 * head
            rows = pl.ds(2 * chunk, 8)
            tops = parts[:, rows, at:at + 1]
            totals = parts[:, rows, at + 1:at + 2]
            top = jnp.max(tops, axis=0, keepdims=True)
            factor = jnp.exp(tops - top)
            total = jnp.sum(totals * factor, axis=0)
            summed = jnp.sum(parts[:, pl.ds(head * chunk + 8 * tile, 8), :] * factor, axis=0)
            out_tile = (summed / total).astype(BF16)
            for t in range(GROUP):
                out[t, pl.ds(8 * tile, 8), head * HEAD_DIM:(head + 1) * HEAD_DIM] = out_tile


def project_kernel(block_ids, attended, vo0, vo1, vo2, vo3, vo4, latents, upd, squares):
    refs = ((vo0, 0, 4), (vo1, 4, 4), (vo2, 8, 4), (vo3, 12, 2), (vo4, 14, 2))
    total = latents[...].astype(F32)
    chunk = latents.shape[0]
    for ref, start, count in refs:
        for at in range(count):
            slot = start + at
            block = block_ids[slot % SIDE * SIDE + slot // SIDE]
            total += jnp.dot(attended[block], ref[at, 1], preferred_element_type=F32)
    upd[...] = total
    square = jnp.sum(total * total, axis=1, keepdims=True)
    lane = lax.broadcasted_iota(jnp.int32, (8, HEAD_DIM), 1)
    packed = jnp.zeros((8, HEAD_DIM), F32)
    for tile in range(chunk // 8):
        packed = jnp.where(lane == tile, square[8 * tile:8 * tile + 8], packed)
    for t in range(GROUP):
        squares[t] = packed


def finish_kernel(width, squares, upd, gain, out):
    total = jnp.sum(squares[...], axis=0)
    chunk = upd.shape[0]
    for tile in range(chunk // 8):
        rows = pl.ds(8 * tile, 8)
        mean_sq = total[:, tile:tile + 1] / width
        u = upd[rows, :]
        normed = gain[...] * u * lax.rsqrt(mean_sq + 1e-05)
        for a in range(GROUP):
            out[a, 0, rows, :] = u.astype(BF16)
            out[a, 1, rows, :] = normed.astype(BF16)


def whole(count):
    return [pl.BlockSpec(memory_space=pltpu.VMEM)] * count


def body(tokens, valid, latents, w_query, w_key, w_value, w_out, gain):
    me = lax.axis_index("agent")
    rows, depth = tokens.shape
    chunk = latents.shape[0] // GROUP
    width = depth * lax.axis_size("tensor")
    both = jnp.concatenate([tokens, latents], axis=0)
    feats = lax.all_gather(both, "tensor", axis=0, tiled=False)
    qk = gather_weights(w_query, w_key, hop_x, hop_y)
    vo = gather_weights(w_value, w_out, hop_y, hop_x)
    qk = [part.reshape(-1, 2, depth, depth) for part in qk]
    vo = [part.reshape(-1, 2, depth, depth) for part in vo]
    y, x = me // SIDE, me % SIDE
    block_ids = jnp.stack(
        [(y + i + SIDE) % SIDE * SIDE + (x + j + SIDE) % SIDE for i in STEPS for j in STEPS]
    ).astype(jnp.int32)
    smem = pl.BlockSpec(memory_space=pltpu.SMEM)
    anywhere = pl.BlockSpec(memory_space=pl.ANY)
    partial = pl.pallas_call(
        attend_kernel,
        out_shape=jax.ShapeDtypeStruct((GROUP, 2 * chunk + 8, HEAD_DIM), F32),
        in_specs=[smem] + [anywhere] * 11 + whole(1),
        out_specs=whole(1)[0],
        scratch_shapes=[
            pltpu.VMEM((GROUP, 2 * rows, depth), BF16),
            pltpu.VMEM((GROUP, 2, depth, depth), BF16),
            pltpu.VMEM((GROUP, depth, depth), BF16),
            pltpu.VMEM((GROUP, chunk // 8, 8, HEAD_DIM), F32),
            pltpu.SemaphoreType.DMA((GROUP,)),
            pltpu.SemaphoreType.DMA((5,)),
            pltpu.SemaphoreType.DMA((5,)),
        ],
        compiler_params=pltpu.CompilerParams(vmem_limit_bytes=40 * 2**20),
        name="attend",
    )(block_ids, feats, *qk, *vo, valid.reshape(1, rows))
    partial = lax.all_to_all(partial, "agent", 0, 0)
    attended = pl.pallas_call(
        combine_kernel,
        out_shape=jax.ShapeDtypeStruct((GROUP, chunk, depth), BF16),
        in_specs=whole(1),
        out_specs=whole(1)[0],
        name="combine",
    )(partial)
    attended = lax.all_to_all(attended, "tensor", 0, 0)
    mine = lax.dynamic_slice_in_dim(latents, me * chunk, chunk, axis=0)
    upd, squares = pl.pallas_call(
        project_kernel,
        out_shape=(jax.ShapeDtypeStruct((chunk, depth), F32),
                   jax.ShapeDtypeStruct((GROUP, 8, HEAD_DIM), F32)),
        in_specs=[smem] + whole(7),
        out_specs=tuple(whole(2)),
        compiler_params=pltpu.CompilerParams(vmem_limit_bytes=40 * 2**20),
        name="project",
    )(block_ids, attended, *vo, mine)
    squares = lax.all_to_all(squares, "tensor", 0, 0)
    out = pl.pallas_call(
        lambda *refs: finish_kernel(width, *refs),
        out_shape=jax.ShapeDtypeStruct((GROUP, 2, chunk, depth), BF16),
        in_specs=whole(3),
        out_specs=whole(1)[0],
        name="finish",
    )(squares, upd, gain.reshape(1, depth))
    out = lax.all_to_all(out, "agent", 0, 0)
    return out[:, 0].reshape(-1, depth), out[:, 1].reshape(-1, depth)


def solution(mesh):
    return jax.shard_map(
        body,
        mesh=mesh,
        in_specs=(
            P("agent", "tensor"),
            P("agent"),
            P(None, "tensor"),
            P("agent", "tensor"),
            P("agent", "tensor"),
            P("agent", "tensor"),
            P("agent", "tensor"),
            P("tensor"),
        ),
        out_specs=(P(None, "tensor"), P(None, "tensor")),
        check_vma=False,
    )
```

```python
import jax
import jax.numpy as jnp
from jax import lax
from jax.experimental import pallas as pl
from jax.experimental.pallas import tpu as pltpu
from jax.sharding import PartitionSpec as P

HEAD_DIM = 128
SIDE = 4
GROUP = 16
STEPS = (0, -1, 1, 2)
BF16 = jnp.bfloat16
F32 = jnp.float32


def hop_x(array, by):
    pairs = [(a, a // SIDE * SIDE + (a + by) % SIDE) for a in range(GROUP)]
    return lax.ppermute(array, "agent", pairs)


def hop_y(array, by):
    pairs = [(a, (a + by * SIDE) % GROUP) for a in range(GROUP)]
    return lax.ppermute(array, "agent", pairs)


def line(block, hop):
    half = block.shape[0] // 2
    low = hop(block, 1)
    high = hop(block, -1)
    far_top = hop(low[:half], 1)
    far_bottom = hop(high[half:], -1)
    near = jnp.concatenate([block, low], axis=0)
    rest = jnp.concatenate([high, far_top, far_bottom], axis=0)
    return near, rest


def gather_weights(first, second, hop_one, hop_two):
    near, rest = line(jnp.concatenate([first, second], axis=0), hop_one)
    near_low = hop_two(near, 1)
    near_high = hop_two(near, -1)
    rest_low = hop_two(rest, 1)
    rest_high = hop_two(rest, -1)
    near_far = hop_two(near_low, 1)
    rest_far = hop_two(rest_high, -1)
    return near, rest, near_low, rest_low, near_high, rest_high, near_far, rest_far


def attend_kernel(block_ids, *refs):
    feats, qk_refs, vo_refs = refs[0], refs[1:9], refs[9:17]
    valid, out, x_all, qk_all, v_all, stat, x_sem, qk_sem, v_sem = refs[17:]
    rows = feats.shape[1] // 2
    depth = feats.shape[2]
    x_copies = []
    for slot in range(GROUP):
        copy = pltpu.make_async_copy(feats.at[block_ids[slot]], x_all.at[slot], x_sem.at[slot])
        x_copies.append(copy)
    qk_copies, v_copies = [], []
    for n in range(8):
        qk_copies.append(pltpu.make_async_copy(
            qk_refs[n], qk_all.at[pl.ds(2 * n, 2)], qk_sem.at[n]))
        v_copies.append(pltpu.make_async_copy(
            vo_refs[n].at[:, 0], v_all.at[pl.ds(2 * n, 2)], v_sem.at[n]))
    for part in range(SIDE):
        for copy in x_copies[part * SIDE:(part + 1) * SIDE] + qk_copies[2 * part:2 * part + 2]:
            copy.start()
    for copy in v_copies:
        copy.start()

    def columns(first, top):
        return jnp.concatenate(
            [x_all[first + j, pl.ds(top, rows), :] for j in range(SIDE)], axis=1)

    query = keys = values = None
    for part in range(SIDE):
        for copy in x_copies[part * SIDE:(part + 1) * SIDE] + qk_copies[2 * part:2 * part + 2]:
            copy.wait()
        w_q = qk_all[pl.ds(part * SIDE, SIDE), 0].reshape(SIDE * depth, -1)
        w_k = qk_all[pl.ds(part * SIDE, SIDE), 1].reshape(SIDE * depth, -1)
        more_q = jnp.dot(columns(part * SIDE, rows), w_q, preferred_element_type=F32)
        more_k = jnp.dot(columns(part * SIDE, 0), w_k, preferred_element_type=F32)
        query = more_q if query is None else query + more_q
        keys = more_k if keys is None else keys + more_k
    for copy in v_copies:
        copy.wait()
    for part in range(SIDE):
        w_v = jnp.concatenate([v_all[j * SIDE + part] for j in range(SIDE)], axis=0)
        more_v = jnp.dot(columns(part * SIDE, 0), w_v, preferred_element_type=F32)
        values = more_v if values is None else values + more_v
    query = query.astype(BF16)
    keys = keys.astype(BF16)
    values = values.astype(BF16)
    scale = 1.0 / HEAD_DIM**0.5
    keep = valid[...] > 0
    lane = lax.broadcasted_iota(jnp.int32, (rows, HEAD_DIM), 1)
    tile = lax.broadcasted_iota(jnp.int32, (rows, HEAD_DIM), 0) // 8 % 4
    packed = jnp.zeros((rows, HEAD_DIM), F32)
    chunk = rows // GROUP
    for head in range(2):
        cols = slice(head * HEAD_DIM, (head + 1) * HEAD_DIM)
        scores = lax.dot_general(query[:, cols], keys[:, cols], (((1,), (1,)), ((), ())),
                                 preferred_element_type=F32) * scale
        scores = jnp.where(keep, scores, jnp.float32(-1000000000.0))
        top = jnp.max(scores, axis=1, keepdims=True)
        expo = jnp.exp(scores - top)
        total = jnp.sum(expo, axis=1, keepdims=True)
        coarse = expo.astype(BF16)
        fine = (expo - coarse.astype(F32)).astype(BF16)
        summed = jnp.dot(coarse, values[:, cols], preferred_element_type=F32)
        summed += jnp.dot(fine, values[:, cols], preferred_element_type=F32)
        out[:, pl.ds(head * chunk, chunk), :] = summed.reshape(GROUP, chunk, HEAD_DIM)
        packed = jnp.where(lane == 4 * tile + 2 * head, top, packed)
        packed = jnp.where(lane == 4 * tile + 2 * head + 1, total, packed)
    stat[...] = packed.reshape(GROUP, chunk // 8, 8, HEAD_DIM)
    out[:, pl.ds(2 * chunk, 8), :] = stat[:, 0] + stat[:, 1] + stat[:, 2] + stat[:, 3]


def combine_kernel(parts, out):
    chunk = out.shape[1]
    for tile in range(chunk // 8):
        for head in range(2):
            at = 4 * tile + 2 * head
            rows = pl.ds(2 * chunk, 8)
            tops = parts[:, rows, at:at + 1]
            totals = parts[:, rows, at + 1:at + 2]
            top = jnp.max(tops, axis=0, keepdims=True)
            factor = jnp.exp(tops - top)
            total = jnp.sum(totals * factor, axis=0)
            summed = jnp.sum(parts[:, pl.ds(head * chunk + 8 * tile, 8), :] * factor, axis=0)
            out_tile = (summed / total).astype(BF16)
            for t in range(GROUP):
                out[t, pl.ds(8 * tile, 8), head * HEAD_DIM:(head + 1) * HEAD_DIM] = out_tile


def project_kernel(block_ids, me, attended, *refs):
    vo_refs, (latents, upd, squares) = refs[:8], refs[8:]
    chunk = upd.shape[0]
    total = latents[pl.ds(pl.multiple_of(me[0] * chunk, chunk), chunk), :].astype(F32)
    for slot in range(GROUP):
        block = block_ids[slot % SIDE * SIDE + slot // SIDE]
        total += jnp.dot(
            attended[block], vo_refs[slot // 2][slot % 2, 1], preferred_element_type=F32)
    upd[...] = total
    square = jnp.sum(total * total, axis=1, keepdims=True)
    lane = lax.broadcasted_iota(jnp.int32, (8, HEAD_DIM), 1)
    packed = jnp.zeros((8, HEAD_DIM), F32)
    for tile in range(chunk // 8):
        packed = jnp.where(lane == tile, square[8 * tile:8 * tile + 8], packed)
    for t in range(GROUP):
        squares[t] = packed


def finish_kernel(width, squares, upd, gain, out):
    total = jnp.sum(squares[...], axis=0)
    chunk = upd.shape[0]
    for tile in range(chunk // 8):
        rows = pl.ds(8 * tile, 8)
        mean_sq = total[:, tile:tile + 1] / width
        u = upd[rows, :]
        normed = gain[...] * u * lax.rsqrt(mean_sq + 1e-05)
        for a in range(GROUP):
            out[a, 0, rows, :] = u.astype(BF16)
            out[a, 1, rows, :] = normed.astype(BF16)


def whole(count):
    return [pl.BlockSpec(memory_space=pltpu.VMEM)] * count


def body(tokens, valid, latents, w_query, w_key, w_value, w_out, gain):
    me = lax.axis_index("agent")
    rows, depth = tokens.shape
    chunk = latents.shape[0] // GROUP
    width = depth * lax.axis_size("tensor")
    both = jnp.concatenate([tokens, latents], axis=0)
    feats = lax.all_gather(both, "tensor", axis=0, tiled=False)
    qk = gather_weights(w_query, w_key, hop_x, hop_y)
    vo = gather_weights(w_value, w_out, hop_y, hop_x)
    qk = [part.reshape(-1, 2, depth, depth) for part in qk]
    vo = [part.reshape(-1, 2, depth, depth) for part in vo]
    y, x = me // SIDE, me % SIDE
    block_ids = jnp.stack(
        [(y + i + SIDE) % SIDE * SIDE + (x + j + SIDE) % SIDE for i in STEPS for j in STEPS]
    ).astype(jnp.int32)
    smem = pl.BlockSpec(memory_space=pltpu.SMEM)
    anywhere = pl.BlockSpec(memory_space=pl.ANY)
    partial = pl.pallas_call(
        attend_kernel,
        out_shape=jax.ShapeDtypeStruct((GROUP, 2 * chunk + 8, HEAD_DIM), F32),
        in_specs=[smem] + [anywhere] * 17 + whole(1),
        out_specs=whole(1)[0],
        scratch_shapes=[
            pltpu.VMEM((GROUP, 2 * rows, depth), BF16),
            pltpu.VMEM((GROUP, 2, depth, depth), BF16),
            pltpu.VMEM((GROUP, depth, depth), BF16),
            pltpu.VMEM((GROUP, chunk // 8, 8, HEAD_DIM), F32),
            pltpu.SemaphoreType.DMA((GROUP,)),
            pltpu.SemaphoreType.DMA((8,)),
            pltpu.SemaphoreType.DMA((8,)),
        ],
        compiler_params=pltpu.CompilerParams(vmem_limit_bytes=60 * 2**20),
        name="attend",
    )(block_ids, feats, *qk, *vo, valid.reshape(1, rows))
    partial = lax.all_to_all(partial, "agent", 0, 0)
    attended = pl.pallas_call(
        combine_kernel,
        out_shape=jax.ShapeDtypeStruct((GROUP, chunk, depth), BF16),
        in_specs=whole(1),
        out_specs=whole(1)[0],
        name="combine",
    )(partial)
    attended = lax.all_to_all(attended, "tensor", 0, 0)
    upd, squares = pl.pallas_call(
        project_kernel,
        out_shape=(jax.ShapeDtypeStruct((chunk, depth), F32),
                   jax.ShapeDtypeStruct((GROUP, 8, HEAD_DIM), F32)),
        in_specs=[smem, smem] + whole(10),
        out_specs=tuple(whole(2)),
        compiler_params=pltpu.CompilerParams(vmem_limit_bytes=40 * 2**20),
        name="project",
    )(block_ids, me.astype(jnp.int32).reshape(1), attended, *vo, latents)
    squares = lax.all_to_all(squares, "tensor", 0, 0)
    out = pl.pallas_call(
        lambda *refs: finish_kernel(width, *refs),
        out_shape=jax.ShapeDtypeStruct((GROUP, 2, chunk, depth), BF16),
        in_specs=whole(3),
        out_specs=whole(1)[0],
        name="finish",
    )(squares, upd, gain.reshape(1, depth))
    out = lax.all_to_all(out, "agent", 0, 0)
    return out[:, 0].reshape(-1, depth), out[:, 1].reshape(-1, depth)


def solution(mesh):
    return jax.shard_map(
        body,
        mesh=mesh,
        in_specs=(
            P("agent", "tensor"),
            P("agent"),
            P(None, "tensor"),
            P("agent", "tensor"),
            P("agent", "tensor"),
            P("agent", "tensor"),
            P("agent", "tensor"),
            P("tensor"),
        ),
        out_specs=(P(None, "tensor"), P(None, "tensor")),
        check_vma=False,
    )
```

```python
import jax
import jax.numpy as jnp
from jax import lax
from jax.experimental import pallas as pl
from jax.experimental.pallas import tpu as pltpu
from jax.sharding import PartitionSpec as P

HEAD_DIM = 128
SIDE = 4
GROUP = 16
STEPS = (0, -1, 1, 2)
BF16 = jnp.bfloat16
F32 = jnp.float32


def pairs(move):
    out = []
    for agent in range(GROUP):
        for tensor in range(GROUP):
            y, x = move(agent // SIDE, agent % SIDE, tensor % 2)
            out.append((agent * GROUP + tensor, (y % SIDE * SIDE + x % SIDE) * GROUP + tensor))
    return out


def first(array, by):
    return lax.ppermute(array, ("agent", "tensor"), pairs(
        lambda y, x, core: (y, x + by) if core == 0 else (y + by, x)))


def second(array, by):
    return lax.ppermute(array, ("agent", "tensor"), pairs(
        lambda y, x, core: (y + by, x) if core == 0 else (y, x + by)))


def other_core(array):
    return lax.ppermute(array, "tensor", [(t, t ^ 1) for t in range(GROUP)])


def gather_weights(*weights):
    block = jnp.concatenate(weights, axis=0)
    half = block.shape[0] // 2
    low = first(block, 1)
    high = first(block, -1)
    far_top = first(block[:half], 2)
    far_bottom = first(block[half:], -2)
    near = jnp.concatenate([block, low], axis=0)
    rest = jnp.concatenate([high, far_top, far_bottom], axis=0)
    near, rest = lax.optimization_barrier((near, rest))
    near_low = second(near, 1)
    rest_high = second(rest, -1)
    rest_low = second(rest, 1)
    near_high = second(near, -1)
    near_far = second(near_low, 1)
    rest_far = second(rest_high, -1)
    parts = near, rest, near_low, rest_low, near_high, rest_high, near_far, rest_far
    return [part.reshape(2, len(weights), *weights[0].shape) for part in parts]


def block_table():
    agent, core = lax.axis_index("agent"), lax.axis_index("tensor") % 2
    y, x = agent // SIDE, agent % SIDE
    table = []
    for i in STEPS:
        for j in STEPS:
            dy, dx = jnp.where(core == 0, i, j), jnp.where(core == 0, j, i)
            table.append((y + dy + SIDE) % SIDE * SIDE + (x + dx + SIDE) % SIDE)
    return jnp.stack(table).astype(jnp.int32)


def attend_kernel(block_ids, feats, *refs):
    w_refs = refs[:8]
    valid, out, x_all, w_all, stat, x_sem, w_sem = refs[8:]
    rows = feats.shape[1] // 2
    depth = feats.shape[2]
    x_copies = [
        pltpu.make_async_copy(feats.at[block_ids[slot]], x_all.at[slot], x_sem.at[slot])
        for slot in range(GROUP)
    ]
    w_copies = [
        pltpu.make_async_copy(
            w_refs[n].at[:, pl.ds(0, 3)], w_all.at[pl.ds(2 * n, 2)], w_sem.at[n])
        for n in range(8)
    ]
    copies = [
        x_copies[part * SIDE:(part + 1) * SIDE] + w_copies[2 * part:2 * part + 2]
        for part in range(SIDE)
    ]
    for part in copies:
        for copy in part:
            copy.start()
    sums = [None] * 3
    for part in range(SIDE):
        for copy in copies[part]:
            copy.wait()
        for n, top in enumerate((rows, 0, 0)):
            left = jnp.concatenate(
                [x_all[part * SIDE + j, pl.ds(top, rows), :] for j in range(SIDE)], axis=1)
            right = w_all[pl.ds(part * SIDE, SIDE), n].reshape(SIDE * depth, -1)
            more = jnp.dot(left, right, preferred_element_type=F32)
            sums[n] = more if sums[n] is None else sums[n] + more
    query, keys, values = sums
    query = query.astype(BF16)
    keys = keys.astype(BF16)
    values = values.astype(BF16)
    scale = 1.0 / HEAD_DIM**0.5
    keep = valid[...] > 0
    lane = lax.broadcasted_iota(jnp.int32, (rows, HEAD_DIM), 1)
    tile = lax.broadcasted_iota(jnp.int32, (rows, HEAD_DIM), 0) // 8 % 4
    packed = jnp.zeros((rows, HEAD_DIM), F32)
    chunk = rows // GROUP
    for head in range(2):
        cols = slice(head * HEAD_DIM, (head + 1) * HEAD_DIM)
        scores = lax.dot_general(query[:, cols], keys[:, cols], (((1,), (1,)), ((), ())),
                                 preferred_element_type=F32) * scale
        scores = jnp.where(keep, scores, jnp.float32(-1000000000.0))
        top = jnp.max(scores, axis=1, keepdims=True)
        expo = jnp.exp(scores - top)
        total = jnp.sum(expo, axis=1, keepdims=True)
        coarse = expo.astype(BF16)
        fine = (expo - coarse.astype(F32)).astype(BF16)
        summed = jnp.dot(coarse, values[:, cols], preferred_element_type=F32)
        summed += jnp.dot(fine, values[:, cols], preferred_element_type=F32)
        out[:, pl.ds(head * chunk, chunk), :] = summed.reshape(GROUP, chunk, HEAD_DIM)
        packed = jnp.where(lane == 4 * tile + 2 * head, top, packed)
        packed = jnp.where(lane == 4 * tile + 2 * head + 1, total, packed)
    stat[...] = packed.reshape(GROUP, chunk // 8, 8, HEAD_DIM)
    out[:, pl.ds(2 * chunk, 8), :] = stat[:, 0] + stat[:, 1] + stat[:, 2] + stat[:, 3]


def combine_kernel(parts, out):
    chunk = out.shape[1]
    for tile in range(chunk // 8):
        for head in range(2):
            at = 4 * tile + 2 * head
            rows = pl.ds(2 * chunk, 8)
            tops = parts[:, rows, at:at + 1]
            totals = parts[:, rows, at + 1:at + 2]
            top = jnp.max(tops, axis=0, keepdims=True)
            factor = jnp.exp(tops - top)
            total = jnp.sum(totals * factor, axis=0)
            summed = jnp.sum(parts[:, pl.ds(head * chunk + 8 * tile, 8), :] * factor, axis=0)
            out_tile = (summed / total).astype(BF16)
            for t in range(out.shape[0]):
                out[t, pl.ds(8 * tile, 8), head * HEAD_DIM:(head + 1) * HEAD_DIM] = out_tile


def project_kernel(block_ids, me, mine, theirs, *refs):
    w_refs, (latents, upd, squares, w_all, w_sem) = refs[:8], refs[8:]
    copies = [
        pltpu.make_async_copy(w_refs[n].at[:, 3], w_all.at[pl.ds(2 * n, 2)], w_sem.at[n])
        for n in range(8)
    ]
    for copy in copies:
        copy.start()
    chunk = upd.shape[0]
    total = latents[pl.ds(pl.multiple_of(me[0] * chunk, chunk), chunk), :].astype(F32)
    for copy in copies:
        copy.wait()
    for slot in range(GROUP):
        block = block_ids[slot]
        left = jnp.where(block % 2 == me[1], mine[block // 2], theirs[block // 2])
        total += jnp.dot(left, w_all[slot], preferred_element_type=F32)
    upd[...] = total
    square = jnp.sum(total * total, axis=1, keepdims=True)
    lane = lax.broadcasted_iota(jnp.int32, (8, HEAD_DIM), 1)
    packed = jnp.zeros((8, HEAD_DIM), F32)
    for tile in range(chunk // 8):
        packed = jnp.where(lane == tile, square[8 * tile:8 * tile + 8], packed)
    for t in range(GROUP):
        squares[t] = packed


def finish_kernel(width, squares, upd, gain, out):
    total = jnp.sum(squares[...], axis=0)
    chunk = upd.shape[0]
    for tile in range(chunk // 8):
        rows = pl.ds(8 * tile, 8)
        mean_sq = total[:, tile:tile + 1] / width
        u = upd[rows, :]
        normed = gain[...] * u * lax.rsqrt(mean_sq + 1e-05)
        for a in range(GROUP):
            out[a, 0, rows, :] = u.astype(BF16)
            out[a, 1, rows, :] = normed.astype(BF16)


def whole(count):
    return [pl.BlockSpec(memory_space=pltpu.VMEM)] * count


def body(tokens, valid, latents, w_query, w_key, w_value, w_out, gain):
    me = lax.axis_index("agent")
    rows, depth = tokens.shape
    chunk = latents.shape[0] // GROUP
    width = depth * lax.axis_size("tensor")
    both = jnp.concatenate([tokens, latents], axis=0)
    feats = lax.all_gather(both, "tensor", axis=0, tiled=False)
    weights = gather_weights(w_query, w_key, w_value, w_out)
    block_ids = block_table()
    place = jnp.stack([me, lax.axis_index("tensor") % 2]).astype(jnp.int32)
    smem = pl.BlockSpec(memory_space=pltpu.SMEM)
    anywhere = pl.BlockSpec(memory_space=pl.ANY)
    partial = pl.pallas_call(
        attend_kernel,
        out_shape=jax.ShapeDtypeStruct((GROUP, 2 * chunk + 8, HEAD_DIM), F32),
        in_specs=[smem] + [anywhere] * 9 + whole(1),
        out_specs=whole(1)[0],
        scratch_shapes=[
            pltpu.VMEM((GROUP, 2 * rows, depth), BF16),
            pltpu.VMEM((GROUP, 3, depth, depth), BF16),
            pltpu.VMEM((GROUP, chunk // 8, 8, HEAD_DIM), F32),
            pltpu.SemaphoreType.DMA((GROUP,)),
            pltpu.SemaphoreType.DMA((8,)),
        ],
        compiler_params=pltpu.CompilerParams(vmem_limit_bytes=60 * 2**20),
        name="attend",
    )(block_ids, feats, *weights, valid.reshape(1, rows))
    partial = lax.all_to_all(partial, "agent", 0, 0)
    attended = pl.pallas_call(
        combine_kernel,
        out_shape=jax.ShapeDtypeStruct((GROUP // 2, chunk, depth), BF16),
        in_specs=whole(1),
        out_specs=whole(1)[0],
        name="combine",
    )(partial)
    same_core = [list(range(core, GROUP, 2)) for core in range(2)]
    attended = lax.all_to_all(attended, "tensor", 0, 0, axis_index_groups=same_core)
    theirs = other_core(attended)
    upd, squares = pl.pallas_call(
        project_kernel,
        out_shape=(jax.ShapeDtypeStruct((chunk, depth), F32),
                   jax.ShapeDtypeStruct((GROUP, 8, HEAD_DIM), F32)),
        in_specs=[smem, smem] + whole(2) + [anywhere] * 8 + whole(1),
        out_specs=tuple(whole(2)),
        scratch_shapes=[
            pltpu.VMEM((GROUP, depth, depth), BF16),
            pltpu.SemaphoreType.DMA((8,)),
        ],
        compiler_params=pltpu.CompilerParams(vmem_limit_bytes=60 * 2**20),
        name="project",
    )(block_ids, place, attended, theirs, *weights, latents)
    squares = lax.all_to_all(squares, "tensor", 0, 0)
    out = pl.pallas_call(
        lambda *refs: finish_kernel(width, *refs),
        out_shape=jax.ShapeDtypeStruct((GROUP, 2, chunk, depth), BF16),
        in_specs=whole(3),
        out_specs=whole(1)[0],
        name="finish",
    )(squares, upd, gain.reshape(1, depth))
    out = lax.all_to_all(out, "agent", 0, 0)
    return out[:, 0].reshape(-1, depth), out[:, 1].reshape(-1, depth)


def solution(mesh):
    return jax.shard_map(
        body,
        mesh=mesh,
        in_specs=(
            P("agent", "tensor"),
            P("agent"),
            P(None, "tensor"),
            P("agent", "tensor"),
            P("agent", "tensor"),
            P("agent", "tensor"),
            P("agent", "tensor"),
            P("tensor"),
        ),
        out_specs=(P(None, "tensor"), P(None, "tensor")),
        check_vma=False,
    )
```

```python
import jax
import jax.numpy as jnp
from jax import lax
from jax.experimental import pallas as pl
from jax.experimental.pallas import tpu as pltpu
from jax.sharding import PartitionSpec as P

HEAD_DIM = 128
SIDE = 4
GROUP = 16
STEPS = (0, -1, 1, 2)
BF16 = jnp.bfloat16
F32 = jnp.float32


def pairs(move):
    out = []
    for agent in range(GROUP):
        for tensor in range(GROUP):
            y, x = move(agent // SIDE, agent % SIDE, tensor % 2)
            out.append((agent * GROUP + tensor, (y % SIDE * SIDE + x % SIDE) * GROUP + tensor))
    return out


def first(array, by):
    return lax.ppermute(array, ("agent", "tensor"), pairs(
        lambda y, x, core: (y, x + by) if core == 0 else (y + by, x)))


def second(array, by):
    return lax.ppermute(array, ("agent", "tensor"), pairs(
        lambda y, x, core: (y + by, x) if core == 0 else (y, x + by)))


def along_z(array):
    return lax.ppermute(array, "tensor", [(t, (t + 2 - 4 * (t % 2)) % GROUP) for t in range(GROUP)])


def other_core(array):
    return lax.ppermute(array, "tensor", [(t, t ^ 1) for t in range(GROUP)])


def gather(own, block):
    half = block.shape[0] // 2
    low = first(block, 1)
    high = first(block, -1)
    far_top = first(block[:half], 2)
    far_bottom = first(block[half:], -2)
    a0, b0 = own, other_core(own)
    a1 = along_z(a0)
    low, high, far_top, far_bottom, a0, b0, a1 = lax.optimization_barrier(
        (low, high, far_top, far_bottom, a0, b0, a1))
    near = jnp.concatenate([block, low], axis=0)
    rest = jnp.concatenate([high, far_top, far_bottom], axis=0)
    near_low = second(near, 1)
    rest_high = second(rest, -1)
    rest_low = second(rest, 1)
    near_high = second(near, -1)
    a2, b1 = along_z(a1), along_z(b0)
    a1s = other_core(a1)
    near_low, rest_high, a1, a1s, a2, b1 = lax.optimization_barrier(
        (near_low, rest_high, a1, a1s, a2, b1))
    near_far = second(near_low, 1)
    rest_far = second(rest_high, -1)
    a3, b2 = along_z(a2), along_z(b1)
    a2s, b1s = other_core(a2), other_core(b1)
    rest_low, near_high, a3, b2, a2s, b1s = lax.optimization_barrier(
        (rest_low, near_high, a3, b2, a2s, b1s))
    a4, b3 = along_z(a3), along_z(b2)
    a3s, b2s = other_core(a3), other_core(b2)
    a4s, b3s = other_core(a4), other_core(b3)
    pieces = [a0, b0, a1, b1, a1s, b1s, a2, b2, a2s, b2s, a3, b3, a3s, b3s, a4, a4s]
    return pieces, [near, rest, near_low, rest_low, near_high, rest_high, near_far, rest_far]


def tables():
    agent, tensor = lax.axis_index("agent"), lax.axis_index("tensor")
    y, x, z, core = agent // SIDE, agent % SIDE, tensor // 2, tensor % 2
    table = []
    for i in STEPS:
        for j in STEPS:
            dy, dx = jnp.where(core == 0, i, j), jnp.where(core == 0, j, i)
            table.append((y + dy + SIDE) % SIDE * SIDE + (x + dx + SIDE) % SIDE)
    chips = GROUP // 2
    back = 2 * core - 1
    for k in range(chips // 2 + 1):
        for way in (1, -1) if 0 < k < chips // 2 else (1,):
            chip = (z + way * back * k + chips) % chips
            turn = core if way == 1 else 1 - core
            table += [2 * chip + turn, 2 * chip + 1 - turn]
    return jnp.stack(table + [agent, core]).astype(jnp.int32)


def attend_kernel(table, *refs):
    x_refs, w_refs = refs[:GROUP], refs[GROUP:GROUP + 8]
    valid, out, x_all, stat, x_sem = refs[GROUP + 8:]
    rows = x_all.shape[1] // 2
    depth = x_all.shape[2]
    copies = [
        pltpu.make_async_copy(x_refs[n], x_all.at[table[GROUP + n]], x_sem.at[n])
        for n in range(GROUP)
    ]
    for copy in copies:
        copy.start()
    for copy in copies:
        copy.wait()
    sums = [None] * 3
    for part in range(SIDE):
        lefts = [x_all.at[table[part * SIDE + j]] for j in range(SIDE)]
        for n, top in enumerate((rows, 0, 0)):
            left = jnp.concatenate([ref[pl.ds(top, rows), :] for ref in lefts], axis=1)
            right = jnp.concatenate(
                [w_refs[2 * part + m][:, n].reshape(2 * depth, -1) for m in range(2)], axis=0)
            more = jnp.dot(left, right, preferred_element_type=F32)
            sums[n] = more if sums[n] is None else sums[n] + more
    query, keys, values = sums
    query = query.astype(BF16)
    keys = keys.astype(BF16)
    values = values.astype(BF16)
    scale = 1.0 / HEAD_DIM**0.5
    keep = valid[...] > 0
    lane = lax.broadcasted_iota(jnp.int32, (rows, HEAD_DIM), 1)
    tile = lax.broadcasted_iota(jnp.int32, (rows, HEAD_DIM), 0) // 8 % 4
    packed = jnp.zeros((rows, HEAD_DIM), F32)
    chunk = rows // GROUP
    for head in range(2):
        cols = slice(head * HEAD_DIM, (head + 1) * HEAD_DIM)
        scores = lax.dot_general(query[:, cols], keys[:, cols], (((1,), (1,)), ((), ())),
                                 preferred_element_type=F32) * scale
        scores = jnp.where(keep, scores, jnp.float32(-1000000000.0))
        top = jnp.max(scores, axis=1, keepdims=True)
        expo = jnp.exp(scores - top)
        total = jnp.sum(expo, axis=1, keepdims=True)
        coarse = expo.astype(BF16)
        fine = (expo - coarse.astype(F32)).astype(BF16)
        summed = jnp.dot(coarse, values[:, cols], preferred_element_type=F32)
        summed += jnp.dot(fine, values[:, cols], preferred_element_type=F32)
        out[:, pl.ds(head * chunk, chunk), :] = summed.reshape(GROUP, chunk, HEAD_DIM)
        packed = jnp.where(lane == 4 * tile + 2 * head, top, packed)
        packed = jnp.where(lane == 4 * tile + 2 * head + 1, total, packed)
    stat[...] = packed.reshape(GROUP, chunk // 8, 8, HEAD_DIM)
    out[:, pl.ds(2 * chunk, 8), :] = stat[:, 0] + stat[:, 1] + stat[:, 2] + stat[:, 3]


def combine_kernel(parts, out):
    chunk = out.shape[1]
    for tile in range(chunk // 8):
        for head in range(2):
            at = 4 * tile + 2 * head
            rows = pl.ds(2 * chunk, 8)
            tops = parts[:, rows, at:at + 1]
            totals = parts[:, rows, at + 1:at + 2]
            top = jnp.max(tops, axis=0, keepdims=True)
            factor = jnp.exp(tops - top)
            total = jnp.sum(totals * factor, axis=0)
            summed = jnp.sum(parts[:, pl.ds(head * chunk + 8 * tile, 8), :] * factor, axis=0)
            out_tile = (summed / total).astype(BF16)
            for t in range(out.shape[0]):
                out[t, pl.ds(8 * tile, 8), head * HEAD_DIM:(head + 1) * HEAD_DIM] = out_tile


def project_kernel(table, mine, theirs, *refs):
    w_refs, (latents, upd, squares, rows, sem) = refs[:8], refs[8:]
    chunk, depth = upd.shape
    agent, core = table[2 * GROUP], table[2 * GROUP + 1]
    copy = pltpu.make_async_copy(
        latents.at[pl.ds(pl.multiple_of(agent * chunk, chunk), chunk)], rows, sem)
    copy.start()
    total = jnp.zeros((chunk, depth), F32)
    for n in range(8):
        lefts = []
        for m in range(2):
            block = table[2 * n + m]
            lefts.append(jnp.where(block % 2 == core, mine[block // 2], theirs[block // 2]))
        total += jnp.dot(jnp.concatenate(lefts, axis=1), w_refs[n][:, 3].reshape(2 * depth, depth),
                         preferred_element_type=F32)
    copy.wait()
    total += rows[...].astype(F32)
    upd[...] = total
    square = jnp.sum(total * total, axis=1, keepdims=True)
    lane = lax.broadcasted_iota(jnp.int32, (8, HEAD_DIM), 1)
    packed = jnp.zeros((8, HEAD_DIM), F32)
    for tile in range(chunk // 8):
        packed = jnp.where(lane == tile, square[8 * tile:8 * tile + 8], packed)
    for t in range(GROUP):
        squares[t] = packed


def finish_kernel(width, squares, upd, gain, out):
    total = jnp.sum(squares[...], axis=0)
    chunk = upd.shape[0]
    for tile in range(chunk // 8):
        rows = pl.ds(8 * tile, 8)
        mean_sq = total[:, tile:tile + 1] / width
        u = upd[rows, :]
        normed = gain[...] * u * lax.rsqrt(mean_sq + 1e-05)
        for a in range(GROUP):
            out[a, 0, rows, :] = u.astype(BF16)
            out[a, 1, rows, :] = normed.astype(BF16)


def whole(count):
    return [pl.BlockSpec(memory_space=pltpu.VMEM)] * count


def body(tokens, valid, latents, w_query, w_key, w_value, w_out, gain):
    rows, depth = tokens.shape
    chunk = latents.shape[0] // GROUP
    width = depth * lax.axis_size("tensor")
    pieces, weights = gather(
        jnp.concatenate([tokens, latents], axis=0),
        jnp.concatenate([w_query, w_key, w_value, w_out], axis=0))
    weights = [part.reshape(2, 4, depth, depth) for part in weights]
    table = tables()
    smem = pl.BlockSpec(memory_space=pltpu.SMEM)
    anywhere = pl.BlockSpec(memory_space=pl.ANY)
    partial = pl.pallas_call(
        attend_kernel,
        out_shape=jax.ShapeDtypeStruct((GROUP, 2 * chunk + 8, HEAD_DIM), F32),
        in_specs=[smem] + [anywhere] * GROUP + whole(9),
        out_specs=whole(1)[0],
        scratch_shapes=[
            pltpu.VMEM((GROUP, 2 * rows, depth), BF16),
            pltpu.VMEM((GROUP, chunk // 8, 8, HEAD_DIM), F32),
            pltpu.SemaphoreType.DMA((GROUP,)),
        ],
        compiler_params=pltpu.CompilerParams(vmem_limit_bytes=24 * 2**20),
        name="attend",
    )(table, *pieces, *weights, valid.reshape(1, rows))
    partial = lax.all_to_all(partial, "agent", 0, 0)
    attended = pl.pallas_call(
        combine_kernel,
        out_shape=jax.ShapeDtypeStruct((GROUP // 2, chunk, depth), BF16),
        in_specs=whole(1),
        out_specs=whole(1)[0],
        name="combine",
    )(partial)
    same_core = [list(range(core, GROUP, 2)) for core in range(2)]
    attended = lax.all_to_all(attended, "tensor", 0, 0, axis_index_groups=same_core)
    theirs = other_core(attended)
    upd, squares = pl.pallas_call(
        project_kernel,
        out_shape=(jax.ShapeDtypeStruct((chunk, depth), F32),
                   jax.ShapeDtypeStruct((GROUP, 8, HEAD_DIM), F32)),
        in_specs=[smem] + whole(10) + [anywhere],
        out_specs=tuple(whole(2)),
        scratch_shapes=[
            pltpu.VMEM((chunk, depth), BF16),
            pltpu.SemaphoreType.DMA,
        ],
        compiler_params=pltpu.CompilerParams(vmem_limit_bytes=16 * 2**20),
        name="project",
    )(table, attended, theirs, *weights, latents)
    squares = lax.all_to_all(squares, "tensor", 0, 0)
    out = pl.pallas_call(
        lambda *refs: finish_kernel(width, *refs),
        out_shape=jax.ShapeDtypeStruct((GROUP, 2, chunk, depth), BF16),
        in_specs=whole(3),
        out_specs=whole(1)[0],
        name="finish",
    )(squares, upd, gain.reshape(1, depth))
    out = lax.all_to_all(out, "agent", 0, 0)
    return out[:, 0].reshape(-1, depth), out[:, 1].reshape(-1, depth)


def solution(mesh):
    return jax.shard_map(
        body,
        mesh=mesh,
        in_specs=(
            P("agent", "tensor"),
            P("agent"),
            P(None, "tensor"),
            P("agent", "tensor"),
            P("agent", "tensor"),
            P("agent", "tensor"),
            P("agent", "tensor"),
            P("tensor"),
        ),
        out_specs=(P(None, "tensor"), P(None, "tensor")),
        check_vma=False,
    )
```

```python
import jax
import jax.numpy as jnp
from jax import lax
from jax.experimental import pallas as pl
from jax.experimental.pallas import tpu as pltpu
from jax.sharding import PartitionSpec as P

HEAD_DIM = 128
SIDE = 4
GROUP = 16
STEPS = (0, -1, 1, 2)
BF16 = jnp.bfloat16
F32 = jnp.float32


def pairs(move):
    out = []
    for agent in range(GROUP):
        for tensor in range(GROUP):
            y, x = move(agent // SIDE, agent % SIDE, tensor % 2)
            out.append((agent * GROUP + tensor, (y % SIDE * SIDE + x % SIDE) * GROUP + tensor))
    return out


def first(array, by):
    return lax.ppermute(array, ("agent", "tensor"), pairs(
        lambda y, x, core: (y, x + by) if core == 0 else (y + by, x)))


def second(array, by):
    return lax.ppermute(array, ("agent", "tensor"), pairs(
        lambda y, x, core: (y + by, x) if core == 0 else (y, x + by)))


def other_core(array):
    return lax.ppermute(array, "tensor", [(t, t ^ 1) for t in range(GROUP)])


def gather_weights(*weights):
    block = jnp.concatenate(weights, axis=0)
    half = block.shape[0] // 2
    low = first(block, 1)
    high = first(block, -1)
    far_top = first(block[:half], 2)
    far_bottom = first(block[half:], -2)
    near = jnp.concatenate([block, low], axis=0)
    rest = jnp.concatenate([high, far_top, far_bottom], axis=0)
    near, rest = lax.optimization_barrier((near, rest))
    near_low = second(near, 1)
    rest_high = second(rest, -1)
    rest_low = second(rest, 1)
    near_high = second(near, -1)
    near_far = second(near_low, 1)
    rest_far = second(rest_high, -1)
    parts = near, rest, near_low, rest_low, near_high, rest_high, near_far, rest_far
    return [part.reshape(2, len(weights), *weights[0].shape) for part in parts]


def index_table():
    agent, core = lax.axis_index("agent"), lax.axis_index("tensor") % 2
    y, x = agent // SIDE, agent % SIDE
    table = []
    for i in STEPS:
        for j in STEPS:
            dy, dx = jnp.where(core == 0, i, j), jnp.where(core == 0, j, i)
            table.append((y + dy + SIDE) % SIDE * SIDE + (x + dx + SIDE) % SIDE)
    return jnp.stack(table + [agent, core]).astype(jnp.int32)


def attend_kernel(table, feats, *refs):
    w_refs = refs[:8]
    valid, out, x_all, w_all, acc, stat, x_sem, w_sem = refs[8:]
    rows = feats.shape[1] // 2
    depth = feats.shape[2]
    parts = 8
    step = GROUP // parts
    copies = [[] for _ in range(parts)]
    for slot in range(GROUP):
        copies[slot // step].append(pltpu.make_async_copy(
            feats.at[table[slot]], x_all.at[:, pl.ds(slot * depth, depth)], x_sem.at[slot]))
    for part in range(2, parts):
        for n in range(3):
            copies[part].append(pltpu.make_async_copy(
                w_refs[part].at[:, n], w_all.at[n, pl.ds(part * step, step)], w_sem.at[n, part]))
    for part in copies:
        for copy in part:
            copy.start()
    sums = [None] * 3
    for part in range(parts):
        for copy in copies[part]:
            copy.wait()
        for n, top in enumerate((rows, 0, 0)):
            left = x_all[pl.ds(top, rows), pl.ds(part * step * depth, step * depth)]
            if part < 2:
                right = w_refs[part][:, n]
            else:
                right = w_all[n, pl.ds(part * step, step)]
            more = jnp.dot(left, right.reshape(step * depth, depth), preferred_element_type=F32)
            if part == 0:
                acc[n] = more
            elif part < parts - 1:
                acc[n] += more
            else:
                sums[n] = acc[n] + more
    query, keys, values = sums
    query = query.astype(BF16)
    keys = keys.astype(BF16)
    values = values.astype(BF16)
    scale = 1.0 / HEAD_DIM**0.5
    keep = valid[...] > 0
    lane = lax.broadcasted_iota(jnp.int32, (rows, HEAD_DIM), 1)
    tile = lax.broadcasted_iota(jnp.int32, (rows, HEAD_DIM), 0) // 8 % 4
    packed = jnp.zeros((rows, HEAD_DIM), F32)
    chunk = rows // GROUP
    for head in range(2):
        cols = slice(head * HEAD_DIM, (head + 1) * HEAD_DIM)
        scores = lax.dot_general(query[:, cols], keys[:, cols], (((1,), (1,)), ((), ())),
                                 preferred_element_type=F32) * scale
        scores = jnp.where(keep, scores, jnp.float32(-1000000000.0))
        top = jnp.max(scores, axis=1, keepdims=True)
        expo = jnp.exp(scores - top)
        total = jnp.sum(expo, axis=1, keepdims=True)
        coarse = expo.astype(BF16)
        fine = (expo - coarse.astype(F32)).astype(BF16)
        summed = jnp.dot(coarse, values[:, cols], preferred_element_type=F32)
        summed += jnp.dot(fine, values[:, cols], preferred_element_type=F32)
        out[:, pl.ds(head * chunk, chunk), :] = summed.reshape(GROUP, chunk, HEAD_DIM)
        packed = jnp.where(lane == 4 * tile + 2 * head, top, packed)
        packed = jnp.where(lane == 4 * tile + 2 * head + 1, total, packed)
    stat[...] = packed.reshape(GROUP, chunk // 8, 8, HEAD_DIM)
    out[:, pl.ds(2 * chunk, 8), :] = stat[:, 0] + stat[:, 1] + stat[:, 2] + stat[:, 3]


def combine_kernel(parts, out):
    chunk = out.shape[1]
    stat = parts[:, pl.ds(2 * chunk, 8), :]
    factor = jnp.exp(stat - jnp.max(stat, axis=0, keepdims=True))
    lane = lax.broadcasted_iota(jnp.int32, (1, 8, HEAD_DIM), 2)
    factor = jnp.where(lane % 2 == 0, factor, 0.0)
    total = jnp.sum(pltpu.roll(factor, 1, 2) * stat, axis=0, keepdims=True)
    factor = factor / jnp.where(lane % 2 == 0, pltpu.roll(total, HEAD_DIM - 1, 2), 1.0)
    heads = []
    for head in range(2):
        tiles = []
        for tile in range(chunk // 8):
            at = 4 * tile + 2 * head
            rows = pl.ds(head * chunk + 8 * tile, 8)
            tiles.append(jnp.sum(parts[:, rows, :] * factor[:, :, at:at + 1], axis=0))
        heads.append(jnp.concatenate(tiles, axis=0))
    attended = jnp.concatenate(heads, axis=1).astype(BF16)
    for t in range(out.shape[0]):
        out[t] = attended


def project_kernel(table, mine, theirs, *refs):
    w_refs, (latents, upd, squares, w_all, rows, w_sem, sem) = refs[:8], refs[8:]
    chunk, depth = upd.shape
    agent, core = table[GROUP], table[GROUP + 1]
    copies = [
        pltpu.make_async_copy(w_refs[n].at[:, 3], w_all.at[pl.ds(2 * n, 2)], w_sem.at[n])
        for n in range(8)
    ]
    for copy in copies:
        copy.start()
    copy = pltpu.make_async_copy(
        latents.at[pl.ds(pl.multiple_of(agent * chunk, chunk), chunk)], rows, sem)
    copy.start()
    lefts = []
    for slot in range(GROUP):
        block = table[slot]
        lefts.append(jnp.where(block % 2 == core, mine[block // 2], theirs[block // 2]))
    for each in copies:
        each.wait()
    total = jnp.dot(jnp.concatenate(lefts, axis=1), w_all[...].reshape(GROUP * depth, depth),
                    preferred_element_type=F32)
    copy.wait()
    total += rows[...].astype(F32)
    upd[...] = total
    square = jnp.sum(total * total, axis=1, keepdims=True)
    lane = lax.broadcasted_iota(jnp.int32, (8, HEAD_DIM), 1)
    packed = jnp.zeros((8, HEAD_DIM), F32)
    for tile in range(chunk // 8):
        packed = jnp.where(lane == tile, square[8 * tile:8 * tile + 8], packed)
    for t in range(GROUP):
        squares[t] = packed


def finish_kernel(width, squares, upd, gain, out):
    total = jnp.sum(squares[...], axis=0)
    chunk = upd.shape[0]
    mean_sq = jnp.concatenate([total[:, n:n + 1] for n in range(chunk // 8)], axis=0) / width
    u = upd[...]
    normed = (gain[...] * u * lax.rsqrt(mean_sq + 1e-05)).astype(BF16)
    u = u.astype(BF16)
    for a in range(GROUP):
        out[a, 0] = u
        out[a, 1] = normed


def whole(count):
    return [pl.BlockSpec(memory_space=pltpu.VMEM)] * count


def body(tokens, valid, latents, w_query, w_key, w_value, w_out, gain):
    rows, depth = tokens.shape
    chunk = latents.shape[0] // GROUP
    width = depth * lax.axis_size("tensor")
    both = jnp.concatenate([tokens, latents], axis=0)
    feats = lax.all_gather(both, "tensor", axis=0, tiled=False)
    weights = gather_weights(w_query, w_key, w_value, w_out)
    table = index_table()
    smem = pl.BlockSpec(memory_space=pltpu.SMEM)
    anywhere = pl.BlockSpec(memory_space=pl.ANY)
    partial = pl.pallas_call(
        attend_kernel,
        out_shape=jax.ShapeDtypeStruct((GROUP, 2 * chunk + 8, HEAD_DIM), F32),
        in_specs=[smem, anywhere] + whole(2) + [anywhere] * 6 + whole(1),
        out_specs=whole(1)[0],
        scratch_shapes=[
            pltpu.VMEM((2 * rows, GROUP * depth), BF16),
            pltpu.VMEM((3, GROUP, depth, depth), BF16),
            pltpu.VMEM((3, rows, depth), F32),
            pltpu.VMEM((GROUP, chunk // 8, 8, HEAD_DIM), F32),
            pltpu.SemaphoreType.DMA((GROUP,)),
            pltpu.SemaphoreType.DMA((3, 8)),
        ],
        compiler_params=pltpu.CompilerParams(vmem_limit_bytes=40 * 2**20),
        name="attend",
    )(table, feats, *weights, valid.reshape(1, rows))
    partial = lax.all_to_all(partial, "agent", 0, 0)
    attended = pl.pallas_call(
        combine_kernel,
        out_shape=jax.ShapeDtypeStruct((GROUP // 2, chunk, depth), BF16),
        in_specs=whole(1),
        out_specs=whole(1)[0],
        name="combine",
    )(partial)
    same_core = [list(range(core, GROUP, 2)) for core in range(2)]
    attended = lax.all_to_all(attended, "tensor", 0, 0, axis_index_groups=same_core)
    theirs = other_core(attended)
    upd, squares = pl.pallas_call(
        project_kernel,
        out_shape=(jax.ShapeDtypeStruct((chunk, depth), F32),
                   jax.ShapeDtypeStruct((GROUP, 8, HEAD_DIM), F32)),
        in_specs=[smem] + whole(2) + [anywhere] * 9,
        out_specs=tuple(whole(2)),
        scratch_shapes=[
            pltpu.VMEM((GROUP, depth, depth), BF16),
            pltpu.VMEM((chunk, depth), BF16),
            pltpu.SemaphoreType.DMA((8,)),
            pltpu.SemaphoreType.DMA,
        ],
        compiler_params=pltpu.CompilerParams(vmem_limit_bytes=60 * 2**20),
        name="project",
    )(table, attended, theirs, *weights, latents)
    squares = lax.all_to_all(squares, "tensor", 0, 0)
    out = pl.pallas_call(
        lambda *refs: finish_kernel(width, *refs),
        out_shape=jax.ShapeDtypeStruct((GROUP, 2, chunk, depth), BF16),
        in_specs=whole(3),
        out_specs=whole(1)[0],
        name="finish",
    )(squares, upd, gain.reshape(1, depth))
    out = lax.all_to_all(out, "agent", 0, 0)
    return out[:, 0].reshape(-1, depth), out[:, 1].reshape(-1, depth)


def solution(mesh):
    return jax.shard_map(
        body,
        mesh=mesh,
        in_specs=(
            P("agent", "tensor"),
            P("agent"),
            P(None, "tensor"),
            P("agent", "tensor"),
            P("agent", "tensor"),
            P("agent", "tensor"),
            P("agent", "tensor"),
            P("tensor"),
        ),
        out_specs=(P(None, "tensor"), P(None, "tensor")),
        check_vma=False,
    )
```

```python
import jax
import jax.numpy as jnp
from jax import lax
from jax.experimental import pallas as pl
from jax.experimental.pallas import tpu as pltpu
from jax.sharding import PartitionSpec as P

HEAD_DIM = 128
SIDE = 4
GROUP = 16
STEPS = (0, -1, 1, 2)
BF16 = jnp.bfloat16
F32 = jnp.float32


def pairs(move):
    out = []
    for agent in range(GROUP):
        for tensor in range(GROUP):
            y, x = move(agent // SIDE, agent % SIDE, tensor % 2)
            out.append((agent * GROUP + tensor, (y % SIDE * SIDE + x % SIDE) * GROUP + tensor))
    return out


def first(array, by):
    return lax.ppermute(array, ("agent", "tensor"), pairs(
        lambda y, x, core: (y, x + by) if core == 0 else (y + by, x)))


def second(array, by):
    return lax.ppermute(array, ("agent", "tensor"), pairs(
        lambda y, x, core: (y + by, x) if core == 0 else (y, x + by)))


def other_core(array):
    return lax.ppermute(array, "tensor", [(t, t ^ 1) for t in range(GROUP)])


def gather_weights(*weights):
    block = jnp.concatenate(weights, axis=0)
    half = block.shape[0] // 2
    low = first(block, 1)
    high = first(block, -1)
    far_top = first(block[:half], 2)
    far_bottom = first(block[half:], -2)
    near = jnp.concatenate([block, low], axis=0)
    rest = jnp.concatenate([high, far_top, far_bottom], axis=0)
    near, rest = lax.optimization_barrier((near, rest))
    near_low = second(near, 1)
    rest_high = second(rest, -1)
    rest_low = second(rest, 1)
    near_high = second(near, -1)
    near_far = second(near_low, 1)
    rest_far = second(rest_high, -1)
    parts = near, rest, near_low, rest_low, near_high, rest_high, near_far, rest_far
    return [part.reshape(2, len(weights), *weights[0].shape) for part in parts]


def index_table():
    agent, core = lax.axis_index("agent"), lax.axis_index("tensor") % 2
    y, x = agent // SIDE, agent % SIDE
    table = []
    for i in STEPS:
        for j in STEPS:
            dy, dx = jnp.where(core == 0, i, j), jnp.where(core == 0, j, i)
            table.append((y + dy + SIDE) % SIDE * SIDE + (x + dx + SIDE) % SIDE)
    return jnp.stack(table + [agent, core]).astype(jnp.int32)


def attend_kernel(table, feats, *refs):
    w_refs = refs[:8]
    valid, out, x_all, w_all, acc, stat, x_sem, w_sem = refs[8:]
    rows = feats.shape[1] // 2
    depth = feats.shape[2]
    parts = 8
    step = GROUP // parts
    copies = [[] for _ in range(parts)]
    for slot in range(GROUP):
        copies[slot // step].append(pltpu.make_async_copy(
            feats.at[table[slot]], x_all.at[:, pl.ds(slot * depth, depth)], x_sem.at[slot]))
    for part in range(2, parts):
        for n in range(3):
            copies[part].append(pltpu.make_async_copy(
                w_refs[part].at[:, n], w_all.at[n, pl.ds(part * step, step)], w_sem.at[n, part]))
    for part in copies:
        for copy in part:
            copy.start()
    sums = [None] * 3
    for part in range(parts):
        for copy in copies[part]:
            copy.wait()
        for n, top in enumerate((rows, 0, 0)):
            left = x_all[pl.ds(top, rows), pl.ds(part * step * depth, step * depth)]
            if part < 2:
                right = w_refs[part][:, n]
            else:
                right = w_all[n, pl.ds(part * step, step)]
            more = jnp.dot(left, right.reshape(step * depth, depth), preferred_element_type=F32)
            if part == 0:
                acc[n] = more
            elif part < parts - 1:
                acc[n] += more
            else:
                sums[n] = acc[n] + more
    query, keys, values = sums
    query = query.astype(BF16)
    keys = keys.astype(BF16)
    values = values.astype(BF16)
    scale = 1.0 / HEAD_DIM**0.5
    keep = valid[...] > 0
    lane = lax.broadcasted_iota(jnp.int32, (rows, HEAD_DIM), 1)
    tile = lax.broadcasted_iota(jnp.int32, (rows, HEAD_DIM), 0) // 8 % 4
    packed = jnp.zeros((rows, HEAD_DIM), F32)
    chunk = rows // GROUP
    for head in range(2):
        cols = slice(head * HEAD_DIM, (head + 1) * HEAD_DIM)
        scores = lax.dot_general(query[:, cols], keys[:, cols], (((1,), (1,)), ((), ())),
                                 preferred_element_type=F32) * scale
        scores = jnp.where(keep, scores, jnp.float32(-1000000000.0))
        top = jnp.max(scores, axis=1, keepdims=True)
        expo = jnp.exp(scores - top)
        total = jnp.sum(expo, axis=1, keepdims=True)
        coarse = expo.astype(BF16)
        fine = (expo - coarse.astype(F32)).astype(BF16)
        summed = jnp.dot(coarse, values[:, cols], preferred_element_type=F32)
        summed += jnp.dot(fine, values[:, cols], preferred_element_type=F32)
        out[:, pl.ds(head * chunk, chunk), :] = summed.reshape(GROUP, chunk, HEAD_DIM)
        packed = jnp.where(lane == 4 * tile + 2 * head, top, packed)
        packed = jnp.where(lane == 4 * tile + 2 * head + 1, total, packed)
    stat[...] = packed.reshape(GROUP, chunk // 8, 8, HEAD_DIM)
    out[:, pl.ds(2 * chunk, 8), :] = stat[:, 0] + stat[:, 1] + stat[:, 2] + stat[:, 3]


def combine_kernel(parts, out):
    chunk = out.shape[1]
    stat = parts[:, pl.ds(2 * chunk, 8), :]
    factor = jnp.exp(stat - jnp.max(stat, axis=0, keepdims=True))
    lane = lax.broadcasted_iota(jnp.int32, (1, 8, HEAD_DIM), 2)
    factor = jnp.where(lane % 2 == 0, factor, 0.0)
    total = jnp.sum(pltpu.roll(factor, 1, 2) * stat, axis=0, keepdims=True)
    factor = factor / jnp.where(lane % 2 == 0, pltpu.roll(total, HEAD_DIM - 1, 2), 1.0)
    heads = []
    for head in range(2):
        tiles = []
        for tile in range(chunk // 8):
            at = 4 * tile + 2 * head
            rows = pl.ds(head * chunk + 8 * tile, 8)
            tiles.append(jnp.sum(parts[:, rows, :] * factor[:, :, at:at + 1], axis=0))
        heads.append(jnp.concatenate(tiles, axis=0))
    attended = jnp.concatenate(heads, axis=1).astype(BF16)
    for t in range(out.shape[0]):
        out[t] = attended


def project_kernel(table, mine, theirs, *refs):
    w_refs, (latents, upd, squares, w_all, rows, w_sem, sem) = refs[:8], refs[8:]
    chunk, depth = upd.shape
    agent, core = table[GROUP], table[GROUP + 1]
    copies = [
        pltpu.make_async_copy(w_refs[n].at[:, 3], w_all.at[pl.ds(2 * n, 2)], w_sem.at[n])
        for n in range(8)
    ]
    for copy in copies:
        copy.start()
    copy = pltpu.make_async_copy(
        latents.at[pl.ds(pl.multiple_of(agent * chunk, chunk), chunk)], rows, sem)
    copy.start()
    lefts = []
    for slot in range(GROUP):
        block = table[slot]
        lefts.append(jnp.where(block % 2 == core, mine[block // 2], theirs[block // 2]))
    for each in copies:
        each.wait()
    total = jnp.dot(jnp.concatenate(lefts, axis=1), w_all[...].reshape(GROUP * depth, depth),
                    preferred_element_type=F32)
    copy.wait()
    total += rows[...].astype(F32)
    upd[...] = total
    square = jnp.sum(total * total, axis=1, keepdims=True)
    lane = lax.broadcasted_iota(jnp.int32, (8, HEAD_DIM), 1)
    packed = jnp.zeros((8, HEAD_DIM), F32)
    for tile in range(chunk // 8):
        packed = jnp.where(lane == tile, square[8 * tile:8 * tile + 8], packed)
    for t in range(GROUP):
        squares[t] = packed


def finish_kernel(width, squares, upd, gain, out):
    total = jnp.sum(squares[...], axis=0)
    chunk = upd.shape[0]
    mean_sq = jnp.concatenate([total[:, n:n + 1] for n in range(chunk // 8)], axis=0) / width
    u = upd[...]
    normed = (gain[...] * u * lax.rsqrt(mean_sq + 1e-05)).astype(BF16)
    u = u.astype(BF16)
    for a in range(GROUP):
        out[a, 0] = u
        out[a, 1] = normed


def whole(count):
    return [pl.BlockSpec(memory_space=pltpu.VMEM)] * count


def body(tokens, valid, latents, w_query, w_key, w_value, w_out, gain):
    rows, depth = tokens.shape
    chunk = latents.shape[0] // GROUP
    width = depth * lax.axis_size("tensor")
    both = jnp.concatenate([tokens, latents], axis=0)
    feats = lax.all_gather(both, "tensor", axis=0, tiled=False)
    weights = gather_weights(w_query, w_key, w_value, w_out)
    table = index_table()
    smem = pl.BlockSpec(memory_space=pltpu.SMEM)
    hbm = pl.BlockSpec(memory_space=pltpu.HBM)
    partial = pl.pallas_call(
        attend_kernel,
        out_shape=jax.ShapeDtypeStruct((GROUP, 2 * chunk + 8, HEAD_DIM), F32),
        in_specs=[smem, hbm] + whole(2) + [hbm] * 6 + whole(1),
        out_specs=whole(1)[0],
        scratch_shapes=[
            pltpu.VMEM((2 * rows, GROUP * depth), BF16),
            pltpu.VMEM((3, GROUP, depth, depth), BF16),
            pltpu.VMEM((3, rows, depth), F32),
            pltpu.VMEM((GROUP, chunk // 8, 8, HEAD_DIM), F32),
            pltpu.SemaphoreType.DMA((GROUP,)),
            pltpu.SemaphoreType.DMA((3, 8)),
        ],
        compiler_params=pltpu.CompilerParams(vmem_limit_bytes=40 * 2**20),
        name="attend",
    )(table, feats, *weights, valid.reshape(1, rows))
    partial = lax.all_to_all(partial, "agent", 0, 0)
    attended = pl.pallas_call(
        combine_kernel,
        out_shape=jax.ShapeDtypeStruct((GROUP // 2, chunk, depth), BF16),
        in_specs=whole(1),
        out_specs=whole(1)[0],
        compiler_params=pltpu.CompilerParams(vmem_limit_bytes=4 * 2**20),
        name="combine",
    )(partial)
    same_core = [list(range(core, GROUP, 2)) for core in range(2)]
    attended = lax.all_to_all(attended, "tensor", 0, 0, axis_index_groups=same_core)
    theirs = other_core(attended)
    upd, squares = pl.pallas_call(
        project_kernel,
        out_shape=(jax.ShapeDtypeStruct((chunk, depth), F32),
                   jax.ShapeDtypeStruct((GROUP, 8, HEAD_DIM), F32)),
        in_specs=[smem] + whole(2) + [hbm] * 9,
        out_specs=tuple(whole(2)),
        scratch_shapes=[
            pltpu.VMEM((GROUP, depth, depth), BF16),
            pltpu.VMEM((chunk, depth), BF16),
            pltpu.SemaphoreType.DMA((8,)),
            pltpu.SemaphoreType.DMA,
        ],
        compiler_params=pltpu.CompilerParams(vmem_limit_bytes=8 * 2**20),
        name="project",
    )(table, attended, theirs, *weights, latents)
    squares = lax.all_to_all(squares, "tensor", 0, 0)
    out = pl.pallas_call(
        lambda *refs: finish_kernel(width, *refs),
        out_shape=jax.ShapeDtypeStruct((GROUP, 2, chunk, depth), BF16),
        in_specs=whole(3),
        out_specs=whole(1)[0],
        compiler_params=pltpu.CompilerParams(vmem_limit_bytes=4 * 2**20),
        name="finish",
    )(squares, upd, gain.reshape(1, depth))
    out = lax.all_to_all(out, "agent", 0, 0)
    return out[:, 0].reshape(-1, depth), out[:, 1].reshape(-1, depth)


def solution(mesh):
    return jax.shard_map(
        body,
        mesh=mesh,
        in_specs=(
            P("agent", "tensor"),
            P("agent"),
            P(None, "tensor"),
            P("agent", "tensor"),
            P("agent", "tensor"),
            P("agent", "tensor"),
            P("agent", "tensor"),
            P("tensor"),
        ),
        out_specs=(P(None, "tensor"), P(None, "tensor")),
        check_vma=False,
    )
```

```python
import jax
import jax.numpy as jnp
from jax import lax
from jax.experimental import pallas as pl
from jax.experimental.pallas import tpu as pltpu
from jax.sharding import PartitionSpec as P

HEAD_DIM = 128
SIDE = 4
GROUP = 16
STEPS = (0, -1, 1, 2)
BF16 = jnp.bfloat16
F32 = jnp.float32


def pairs(move):
    out = []
    for agent in range(GROUP):
        for tensor in range(GROUP):
            y, x = move(agent // SIDE, agent % SIDE, tensor % 2)
            out.append((agent * GROUP + tensor, (y % SIDE * SIDE + x % SIDE) * GROUP + tensor))
    return out


def first(array, by):
    return lax.ppermute(array, ("agent", "tensor"), pairs(
        lambda y, x, core: (y, x + by) if core == 0 else (y + by, x)))


def second(array, by):
    return lax.ppermute(array, ("agent", "tensor"), pairs(
        lambda y, x, core: (y + by, x) if core == 0 else (y, x + by)))


def other_core(array):
    return lax.ppermute(array, "tensor", [(t, t ^ 1) for t in range(GROUP)])


def gather_weights(*weights):
    block = jnp.concatenate(weights, axis=0)
    half = block.shape[0] // 2
    low = first(block, 1)
    high = first(block, -1)
    far_top = first(block[:half], 2)
    far_bottom = first(block[half:], -2)
    near = jnp.concatenate([block, low], axis=0)
    rest = jnp.concatenate([high, far_top, far_bottom], axis=0)
    near, rest = lax.optimization_barrier((near, rest))
    near_low = second(near, 1)
    rest_high = second(rest, -1)
    rest_low = second(rest, 1)
    near_high = second(near, -1)
    near_far = second(near_low, 1)
    rest_far = second(rest_high, -1)
    parts = near, rest, near_low, rest_low, near_high, rest_high, near_far, rest_far
    return [part.reshape(2, len(weights), *weights[0].shape) for part in parts]


def index_table():
    agent, core = lax.axis_index("agent"), lax.axis_index("tensor") % 2
    y, x = agent // SIDE, agent % SIDE
    table = []
    for i in STEPS:
        for j in STEPS:
            dy, dx = jnp.where(core == 0, i, j), jnp.where(core == 0, j, i)
            table.append((y + dy + SIDE) % SIDE * SIDE + (x + dx + SIDE) % SIDE)
    return jnp.stack(table + [agent, core]).astype(jnp.int32)


def attend_kernel(table, feats, *refs):
    w_refs = refs[:8]
    valid, out, w_out, x_all, w_all, acc, stat, x_sem, w_sem, out_sem = refs[8:]
    rows = feats.shape[1] // 2
    depth = feats.shape[2]
    parts = 8
    step = GROUP // parts
    copies = [[] for _ in range(parts)]
    for slot in range(GROUP):
        copies[slot // step].append(pltpu.make_async_copy(
            feats.at[table[slot]], x_all.at[:, pl.ds(slot * depth, depth)], x_sem.at[slot]))
    for part in range(2, parts):
        for n in range(3):
            copies[part].append(pltpu.make_async_copy(
                w_refs[part].at[:, n], w_all.at[n, pl.ds(part * step, step)], w_sem.at[n, part]))
    for part in copies:
        for copy in part:
            copy.start()
    out_copies = [
        pltpu.make_async_copy(
            w_refs[n].at[:, 3], w_out.at[pl.ds(n * step, step)], out_sem.at[n])
        for n in range(2, parts)
    ]
    for copy in out_copies:
        copy.start()
    for n in range(2):
        w_out[pl.ds(n * step, step)] = w_refs[n][:, 3]
    sums = [None] * 3
    for part in range(parts):
        for copy in copies[part]:
            copy.wait()
        for n, top in enumerate((rows, 0, 0)):
            left = x_all[pl.ds(top, rows), pl.ds(part * step * depth, step * depth)]
            if part < 2:
                right = w_refs[part][:, n]
            else:
                right = w_all[n, pl.ds(part * step, step)]
            more = jnp.dot(left, right.reshape(step * depth, depth), preferred_element_type=F32)
            if part == 0:
                acc[n] = more
            elif part < parts - 1:
                acc[n] += more
            else:
                sums[n] = acc[n] + more
    query, keys, values = sums
    query = query.astype(BF16)
    keys = keys.astype(BF16)
    values = values.astype(BF16)
    scale = 1.0 / HEAD_DIM**0.5
    keep = valid[...] > 0
    lane = lax.broadcasted_iota(jnp.int32, (rows, HEAD_DIM), 1)
    tile = lax.broadcasted_iota(jnp.int32, (rows, HEAD_DIM), 0) // 8 % 4
    packed = jnp.zeros((rows, HEAD_DIM), F32)
    chunk = rows // GROUP
    for head in range(2):
        cols = slice(head * HEAD_DIM, (head + 1) * HEAD_DIM)
        scores = lax.dot_general(query[:, cols], keys[:, cols], (((1,), (1,)), ((), ())),
                                 preferred_element_type=F32) * scale
        scores = jnp.where(keep, scores, jnp.float32(-1000000000.0))
        top = jnp.max(scores, axis=1, keepdims=True)
        expo = jnp.exp(scores - top)
        total = jnp.sum(expo, axis=1, keepdims=True)
        coarse = expo.astype(BF16)
        fine = (expo - coarse.astype(F32)).astype(BF16)
        summed = jnp.dot(coarse, values[:, cols], preferred_element_type=F32)
        summed += jnp.dot(fine, values[:, cols], preferred_element_type=F32)
        out[:, pl.ds(head * chunk, chunk), :] = summed.reshape(GROUP, chunk, HEAD_DIM)
        packed = jnp.where(lane == 4 * tile + 2 * head, top, packed)
        packed = jnp.where(lane == 4 * tile + 2 * head + 1, total, packed)
    stat[...] = packed.reshape(GROUP, chunk // 8, 8, HEAD_DIM)
    out[:, pl.ds(2 * chunk, 8), :] = stat[:, 0] + stat[:, 1] + stat[:, 2] + stat[:, 3]
    for copy in out_copies:
        copy.wait()


def combine_kernel(parts, out):
    chunk = out.shape[1]
    stat = parts[:, pl.ds(2 * chunk, 8), :]
    factor = jnp.exp(stat - jnp.max(stat, axis=0, keepdims=True))
    lane = lax.broadcasted_iota(jnp.int32, (1, 8, HEAD_DIM), 2)
    factor = jnp.where(lane % 2 == 0, factor, 0.0)
    total = jnp.sum(pltpu.roll(factor, 1, 2) * stat, axis=0, keepdims=True)
    factor = factor / jnp.where(lane % 2 == 0, pltpu.roll(total, HEAD_DIM - 1, 2), 1.0)
    heads = []
    for head in range(2):
        tiles = []
        for tile in range(chunk // 8):
            at = 4 * tile + 2 * head
            rows = pl.ds(head * chunk + 8 * tile, 8)
            tiles.append(jnp.sum(parts[:, rows, :] * factor[:, :, at:at + 1], axis=0))
        heads.append(jnp.concatenate(tiles, axis=0))
    attended = jnp.concatenate(heads, axis=1).astype(BF16)
    for t in range(out.shape[0]):
        out[t] = attended


def project_kernel(table, mine, theirs, w_out, latents, upd, squares, rows, sem):
    chunk, depth = upd.shape
    agent, core = table[GROUP], table[GROUP + 1]
    copy = pltpu.make_async_copy(
        latents.at[pl.ds(pl.multiple_of(agent * chunk, chunk), chunk)], rows, sem)
    copy.start()
    lefts = []
    for slot in range(GROUP):
        block = table[slot]
        lefts.append(jnp.where(block % 2 == core, mine[block // 2], theirs[block // 2]))
    total = jnp.dot(jnp.concatenate(lefts, axis=1), w_out[...].reshape(GROUP * depth, depth),
                    preferred_element_type=F32)
    copy.wait()
    total += rows[...].astype(F32)
    upd[...] = total
    square = jnp.sum(total * total, axis=1, keepdims=True)
    lane = lax.broadcasted_iota(jnp.int32, (8, HEAD_DIM), 1)
    packed = jnp.zeros((8, HEAD_DIM), F32)
    for tile in range(chunk // 8):
        packed = jnp.where(lane == tile, square[8 * tile:8 * tile + 8], packed)
    for t in range(GROUP):
        squares[t] = packed


def finish_kernel(width, squares, upd, gain, out):
    total = jnp.sum(squares[...], axis=0)
    chunk = upd.shape[0]
    mean_sq = jnp.concatenate([total[:, n:n + 1] for n in range(chunk // 8)], axis=0) / width
    u = upd[...]
    normed = (gain[...] * u * lax.rsqrt(mean_sq + 1e-05)).astype(BF16)
    u = u.astype(BF16)
    for a in range(GROUP):
        out[a, 0] = u
        out[a, 1] = normed


def whole(count):
    return [pl.BlockSpec(memory_space=pltpu.VMEM)] * count


def body(tokens, valid, latents, w_query, w_key, w_value, w_out, gain):
    rows, depth = tokens.shape
    chunk = latents.shape[0] // GROUP
    width = depth * lax.axis_size("tensor")
    both = jnp.concatenate([tokens, latents], axis=0)
    feats = lax.all_gather(both, "tensor", axis=0, tiled=False)
    weights = gather_weights(w_query, w_key, w_value, w_out)
    table = index_table()
    smem = pl.BlockSpec(memory_space=pltpu.SMEM)
    hbm = pl.BlockSpec(memory_space=pltpu.HBM)
    partial, out_weight = pl.pallas_call(
        attend_kernel,
        out_shape=(jax.ShapeDtypeStruct((GROUP, 2 * chunk + 8, HEAD_DIM), F32),
                   jax.ShapeDtypeStruct((GROUP, depth, depth), BF16)),
        in_specs=[smem, hbm] + whole(2) + [hbm] * 6 + whole(1),
        out_specs=tuple(whole(2)),
        scratch_shapes=[
            pltpu.VMEM((2 * rows, GROUP * depth), BF16),
            pltpu.VMEM((3, GROUP, depth, depth), BF16),
            pltpu.VMEM((3, rows, depth), F32),
            pltpu.VMEM((GROUP, chunk // 8, 8, HEAD_DIM), F32),
            pltpu.SemaphoreType.DMA((GROUP,)),
            pltpu.SemaphoreType.DMA((3, 8)),
            pltpu.SemaphoreType.DMA((8,)),
        ],
        compiler_params=pltpu.CompilerParams(vmem_limit_bytes=40 * 2**20),
        name="attend",
    )(table, feats, *weights, valid.reshape(1, rows))
    partial = lax.all_to_all(partial, "agent", 0, 0)
    attended = pl.pallas_call(
        combine_kernel,
        out_shape=jax.ShapeDtypeStruct((GROUP // 2, chunk, depth), BF16),
        in_specs=whole(1),
        out_specs=whole(1)[0],
        compiler_params=pltpu.CompilerParams(vmem_limit_bytes=4 * 2**20),
        name="combine",
    )(partial)
    same_core = [list(range(core, GROUP, 2)) for core in range(2)]
    attended = lax.all_to_all(attended, "tensor", 0, 0, axis_index_groups=same_core)
    theirs = other_core(attended)
    upd, squares = pl.pallas_call(
        project_kernel,
        out_shape=(jax.ShapeDtypeStruct((chunk, depth), F32),
                   jax.ShapeDtypeStruct((GROUP, 8, HEAD_DIM), F32)),
        in_specs=[smem] + whole(3) + [hbm],
        out_specs=tuple(whole(2)),
        scratch_shapes=[
            pltpu.VMEM((chunk, depth), BF16),
            pltpu.SemaphoreType.DMA,
        ],
        compiler_params=pltpu.CompilerParams(vmem_limit_bytes=8 * 2**20),
        name="project",
    )(table, attended, theirs, out_weight, latents)
    squares = lax.all_to_all(squares, "tensor", 0, 0)
    out = pl.pallas_call(
        lambda *refs: finish_kernel(width, *refs),
        out_shape=jax.ShapeDtypeStruct((GROUP, 2, chunk, depth), BF16),
        in_specs=whole(3),
        out_specs=whole(1)[0],
        compiler_params=pltpu.CompilerParams(vmem_limit_bytes=4 * 2**20),
        name="finish",
    )(squares, upd, gain.reshape(1, depth))
    out = lax.all_to_all(out, "agent", 0, 0)
    return out[:, 0].reshape(-1, depth), out[:, 1].reshape(-1, depth)


def solution(mesh):
    return jax.shard_map(
        body,
        mesh=mesh,
        in_specs=(
            P("agent", "tensor"),
            P("agent"),
            P(None, "tensor"),
            P("agent", "tensor"),
            P("agent", "tensor"),
            P("agent", "tensor"),
            P("agent", "tensor"),
            P("tensor"),
        ),
        out_specs=(P(None, "tensor"), P(None, "tensor")),
        check_vma=False,
    )
```

```python
import jax
import jax.numpy as jnp
from jax import lax
from jax.experimental import pallas as pl
from jax.experimental.pallas import tpu as pltpu
from jax.sharding import PartitionSpec as P

HEAD_DIM = 128
SIDE = 4
GROUP = 16
STEPS = (0, -1, 1, 2)
BF16 = jnp.bfloat16
F32 = jnp.float32


def pairs(move):
    out = []
    for agent in range(GROUP):
        for tensor in range(GROUP):
            y, x = move(agent // SIDE, agent % SIDE, tensor % 2)
            out.append((agent * GROUP + tensor, (y % SIDE * SIDE + x % SIDE) * GROUP + tensor))
    return out


def first(array, by):
    return lax.ppermute(array, ("agent", "tensor"), pairs(
        lambda y, x, core: (y, x + by) if core == 0 else (y + by, x)))


def second(array, by):
    return lax.ppermute(array, ("agent", "tensor"), pairs(
        lambda y, x, core: (y + by, x) if core == 0 else (y, x + by)))


def other_core(array):
    return lax.ppermute(array, "tensor", [(t, t ^ 1) for t in range(GROUP)])


def gather_weights(*weights):
    block = jnp.concatenate(weights, axis=0)
    half = block.shape[0] // 2
    low = first(block, 1)
    high = first(block, -1)
    far_top = first(block[:half], 2)
    far_bottom = first(block[half:], -2)
    near = jnp.concatenate([block, low], axis=0)
    rest = jnp.concatenate([high, far_top, far_bottom], axis=0)
    near, rest = lax.optimization_barrier((near, rest))
    near_low = second(near, 1)
    rest_high = second(rest, -1)
    rest_low = second(rest, 1)
    near_high = second(near, -1)
    near_far = second(near_low, 1)
    rest_far = second(rest_high, -1)
    parts = near, rest, near_low, rest_low, near_high, rest_high, near_far, rest_far
    return [part.reshape(2, len(weights), *weights[0].shape) for part in parts]


def index_table():
    agent, core = lax.axis_index("agent"), lax.axis_index("tensor") % 2
    y, x = agent // SIDE, agent % SIDE
    table = []
    for i in STEPS:
        for j in STEPS:
            dy, dx = jnp.where(core == 0, i, j), jnp.where(core == 0, j, i)
            table.append((y + dy + SIDE) % SIDE * SIDE + (x + dx + SIDE) % SIDE)
    return jnp.stack(table + [agent, core]).astype(jnp.int32)


def attend_kernel(table, feats, *refs):
    w_refs = refs[:8]
    valid, out, w_out, x_all, w_all, acc, stat, x_sem, w_sem, out_sem = refs[8:]
    rows = feats.shape[1] // 2
    depth = feats.shape[2]
    parts = 8
    step = GROUP // parts
    copies = [[] for _ in range(parts)]
    for slot in range(GROUP):
        copies[slot // step].append(pltpu.make_async_copy(
            feats.at[table[slot]], x_all.at[:, pl.ds(slot * depth, depth)], x_sem.at[slot]))
    for part in range(2, parts):
        for n in range(3):
            copies[part].append(pltpu.make_async_copy(
                w_refs[part].at[:, n], w_all.at[n, pl.ds(part * step, step)], w_sem.at[n, part]))
    for part in copies:
        for copy in part:
            copy.start()
    out_copies = [
        pltpu.make_async_copy(
            w_refs[n].at[:, 3], w_out.at[pl.ds(n * step, step)], out_sem.at[n])
        for n in range(2, parts)
    ]
    for copy in out_copies:
        copy.start()
    for n in range(2):
        w_out[pl.ds(n * step, step)] = w_refs[n][:, 3]
    sums = [None] * 3
    for part in range(parts):
        for copy in copies[part]:
            copy.wait()
        for n, top in enumerate((rows, 0, 0)):
            left = x_all[pl.ds(top, rows), pl.ds(part * step * depth, step * depth)]
            if part < 2:
                right = w_refs[part][:, n]
            else:
                right = w_all[n, pl.ds(part * step, step)]
            more = jnp.dot(left, right.reshape(step * depth, depth), preferred_element_type=F32)
            if part == 0:
                acc[n] = more
            elif part < parts - 1:
                acc[n] += more
            else:
                sums[n] = acc[n] + more
    query, keys, values = sums
    query = query.astype(BF16)
    keys = keys.astype(BF16)
    values = values.astype(BF16)
    scale = 1.0 / HEAD_DIM**0.5
    keep = valid[...] > 0
    lane = lax.broadcasted_iota(jnp.int32, (rows, HEAD_DIM), 1)
    tile = lax.broadcasted_iota(jnp.int32, (rows, HEAD_DIM), 0) // 8 % 4
    packed = jnp.zeros((rows, HEAD_DIM), F32)
    chunk = rows // GROUP
    for head in range(2):
        cols = slice(head * HEAD_DIM, (head + 1) * HEAD_DIM)
        scores = lax.dot_general(query[:, cols], keys[:, cols], (((1,), (1,)), ((), ())),
                                 preferred_element_type=F32) * scale
        scores = jnp.where(keep, scores, jnp.float32(-1000000000.0))
        top = jnp.max(scores, axis=1, keepdims=True)
        expo = jnp.exp(scores - top)
        total = jnp.sum(expo, axis=1, keepdims=True)
        coarse = expo.astype(BF16)
        fine = (expo - coarse.astype(F32)).astype(BF16)
        summed = jnp.dot(coarse, values[:, cols], preferred_element_type=F32)
        summed += jnp.dot(fine, values[:, cols], preferred_element_type=F32)
        out[:, pl.ds(head * chunk, chunk), :] = summed.reshape(GROUP, chunk, HEAD_DIM)
        packed = jnp.where(lane == 4 * tile + 2 * head, top, packed)
        packed = jnp.where(lane == 4 * tile + 2 * head + 1, total, packed)
    stat[...] = packed.reshape(GROUP, chunk // 8, 8, HEAD_DIM)
    out[:, pl.ds(2 * chunk, 8), :] = stat[:, 0] + stat[:, 1] + stat[:, 2] + stat[:, 3]
    for copy in out_copies:
        copy.wait()


def combine_kernel(parts, out):
    chunk = out.shape[1]
    stat = parts[:, pl.ds(2 * chunk, 8), :]
    factor = jnp.exp(stat - jnp.max(stat, axis=0, keepdims=True))
    lane = lax.broadcasted_iota(jnp.int32, (1, 8, HEAD_DIM), 2)
    factor = jnp.where(lane % 2 == 0, factor, 0.0)
    total = jnp.sum(pltpu.roll(factor, 1, 2) * stat, axis=0, keepdims=True)
    factor = factor / jnp.where(lane % 2 == 0, pltpu.roll(total, HEAD_DIM - 1, 2), 1.0)
    heads = []
    for head in range(2):
        tiles = []
        for tile in range(chunk // 8):
            at = 4 * tile + 2 * head
            rows = pl.ds(head * chunk + 8 * tile, 8)
            tiles.append(jnp.sum(parts[:, rows, :] * factor[:, :, at:at + 1], axis=0))
        heads.append(jnp.concatenate(tiles, axis=0))
    attended = jnp.concatenate(heads, axis=1).astype(BF16)
    for t in range(out.shape[0]):
        out[t] = attended


def project_kernel(table, mine, theirs, w_out, latents, upd, squares, rows, sem):
    chunk, depth = upd.shape
    agent, core = table[GROUP], table[GROUP + 1]
    copy = pltpu.make_async_copy(
        latents.at[pl.ds(pl.multiple_of(agent * chunk, chunk), chunk)], rows, sem)
    copy.start()
    lefts = []
    for slot in range(GROUP):
        block = table[slot]
        lefts.append(jnp.where(block % 2 == core, mine[block // 2], theirs[block // 2]))
    total = jnp.dot(jnp.concatenate(lefts, axis=1), w_out[...].reshape(GROUP * depth, depth),
                    preferred_element_type=F32)
    copy.wait()
    total += rows[...].astype(F32)
    upd[...] = total
    square = jnp.sum(total * total, axis=1, keepdims=True)
    lane = lax.broadcasted_iota(jnp.int32, (8, HEAD_DIM), 1)
    packed = jnp.zeros((8, HEAD_DIM), F32)
    for tile in range(chunk // 8):
        packed = jnp.where(lane == tile, square[8 * tile:8 * tile + 8], packed)
    for t in range(GROUP):
        squares[t] = packed


def finish_kernel(width, squares, upd, gain, out):
    total = jnp.sum(squares[...], axis=0)
    chunk, depth = upd.shape
    mean_sq = jnp.concatenate([total[:, n:n + 1] for n in range(chunk // 8)], axis=0) / width
    u = upd[...]
    normed = (gain[...] * u * lax.rsqrt(mean_sq + 1e-05)).astype(BF16)
    u = u.astype(BF16)
    for a in range(GROUP):
        out[a, :, pl.ds(0, depth)] = u
        out[a, :, pl.ds(depth, depth)] = normed


def whole(count):
    return [pl.BlockSpec(memory_space=pltpu.VMEM)] * count


def body(tokens, valid, latents, w_query, w_key, w_value, w_out, gain):
    rows, depth = tokens.shape
    chunk = latents.shape[0] // GROUP
    width = depth * lax.axis_size("tensor")
    both = jnp.concatenate([tokens, latents], axis=0)
    feats = lax.all_gather(both, "tensor", axis=0, tiled=False)
    weights = gather_weights(w_query, w_key, w_value, w_out)
    table = index_table()
    smem = pl.BlockSpec(memory_space=pltpu.SMEM)
    hbm = pl.BlockSpec(memory_space=pltpu.HBM)
    partial, out_weight = pl.pallas_call(
        attend_kernel,
        out_shape=(jax.ShapeDtypeStruct((GROUP, 2 * chunk + 8, HEAD_DIM), F32),
                   jax.ShapeDtypeStruct((GROUP, depth, depth), BF16)),
        in_specs=[smem, hbm] + whole(2) + [hbm] * 6 + whole(1),
        out_specs=tuple(whole(2)),
        scratch_shapes=[
            pltpu.VMEM((2 * rows, GROUP * depth), BF16),
            pltpu.VMEM((3, GROUP, depth, depth), BF16),
            pltpu.VMEM((3, rows, depth), F32),
            pltpu.VMEM((GROUP, chunk // 8, 8, HEAD_DIM), F32),
            pltpu.SemaphoreType.DMA((GROUP,)),
            pltpu.SemaphoreType.DMA((3, 8)),
            pltpu.SemaphoreType.DMA((8,)),
        ],
        compiler_params=pltpu.CompilerParams(vmem_limit_bytes=40 * 2**20),
        name="attend",
    )(table, feats, *weights, valid.reshape(1, rows))
    partial = lax.all_to_all(partial, "agent", 0, 0)
    attended = pl.pallas_call(
        combine_kernel,
        out_shape=jax.ShapeDtypeStruct((GROUP // 2, chunk, depth), BF16),
        in_specs=whole(1),
        out_specs=whole(1)[0],
        compiler_params=pltpu.CompilerParams(vmem_limit_bytes=4 * 2**20),
        name="combine",
    )(partial)
    same_core = [list(range(core, GROUP, 2)) for core in range(2)]
    attended = lax.all_to_all(attended, "tensor", 0, 0, axis_index_groups=same_core)
    theirs = other_core(attended)
    upd, squares = pl.pallas_call(
        project_kernel,
        out_shape=(jax.ShapeDtypeStruct((chunk, depth), F32),
                   jax.ShapeDtypeStruct((GROUP, 8, HEAD_DIM), F32)),
        in_specs=[smem] + whole(3) + [hbm],
        out_specs=tuple(whole(2)),
        scratch_shapes=[
            pltpu.VMEM((chunk, depth), BF16),
            pltpu.SemaphoreType.DMA,
        ],
        compiler_params=pltpu.CompilerParams(vmem_limit_bytes=8 * 2**20),
        name="project",
    )(table, attended, theirs, out_weight, latents)
    squares = lax.all_to_all(squares, "tensor", 0, 0)
    out = pl.pallas_call(
        lambda *refs: finish_kernel(width, *refs),
        out_shape=jax.ShapeDtypeStruct((GROUP, chunk, 2 * depth), BF16),
        in_specs=whole(3),
        out_specs=whole(1)[0],
        compiler_params=pltpu.CompilerParams(vmem_limit_bytes=4 * 2**20),
        name="finish",
    )(squares, upd, gain.reshape(1, depth))
    out = lax.all_to_all(out, "agent", 0, 0)
    return out[:, :, :depth].reshape(-1, depth), out[:, :, depth:].reshape(-1, depth)


def solution(mesh):
    return jax.shard_map(
        body,
        mesh=mesh,
        in_specs=(
            P("agent", "tensor"),
            P("agent"),
            P(None, "tensor"),
            P("agent", "tensor"),
            P("agent", "tensor"),
            P("agent", "tensor"),
            P("agent", "tensor"),
            P("tensor"),
        ),
        out_specs=(P(None, "tensor"), P(None, "tensor")),
        check_vma=False,
    )
```

```python
import jax
import jax.numpy as jnp
from jax import lax
from jax.experimental import pallas as pl
from jax.experimental.pallas import tpu as pltpu
from jax.sharding import PartitionSpec as P

HEAD_DIM = 128
SIDE = 4
GROUP = 16
STEPS = (0, -1, 1, 2)
BF16 = jnp.bfloat16
F32 = jnp.float32


def pairs(move):
    out = []
    for agent in range(GROUP):
        for tensor in range(GROUP):
            y, x = move(agent // SIDE, agent % SIDE, tensor % 2)
            out.append((agent * GROUP + tensor, (y % SIDE * SIDE + x % SIDE) * GROUP + tensor))
    return out


def first(array, by):
    return lax.ppermute(array, ("agent", "tensor"), pairs(
        lambda y, x, core: (y, x + by) if core == 0 else (y + by, x)))


def second(array, by):
    return lax.ppermute(array, ("agent", "tensor"), pairs(
        lambda y, x, core: (y + by, x) if core == 0 else (y, x + by)))


def other_core(array):
    return lax.ppermute(array, "tensor", [(t, t ^ 1) for t in range(GROUP)])


def gather_weights(*weights):
    block = jnp.concatenate(weights, axis=0)
    half = block.shape[0] // 2
    low = first(block, 1)
    high = first(block, -1)
    far_top = first(block[:half], 2)
    far_bottom = first(block[half:], -2)
    near = jnp.concatenate([block, low], axis=0)
    rest = jnp.concatenate([high, far_top, far_bottom], axis=0)
    near, rest = lax.optimization_barrier((near, rest))
    near_low = second(near, 1)
    rest_high = second(rest, -1)
    rest_low = second(rest, 1)
    near_high = second(near, -1)
    near_far = second(near_low, 1)
    rest_far = second(rest_high, -1)
    parts = near, rest, near_low, rest_low, near_high, rest_high, near_far, rest_far
    return [part.reshape(2, len(weights), *weights[0].shape) for part in parts]


def index_table():
    agent, core = lax.axis_index("agent"), lax.axis_index("tensor") % 2
    y, x = agent // SIDE, agent % SIDE
    table = []
    for i in STEPS:
        for j in STEPS:
            dy, dx = jnp.where(core == 0, i, j), jnp.where(core == 0, j, i)
            table.append((y + dy + SIDE) % SIDE * SIDE + (x + dx + SIDE) % SIDE)
    return jnp.stack(table + [agent, core]).astype(jnp.int32)


def attend_kernel(table, feats, *refs):
    w_refs = refs[:8]
    valid, latents, out, w_out, mine, x_all, w_all, acc, stat, x_sem, w_sem, out_sem, mine_sem = refs[8:]
    rows = feats.shape[1] // 2
    depth = feats.shape[2]
    parts = 8
    step = GROUP // parts
    copies = [[] for _ in range(parts)]
    for slot in range(GROUP):
        copies[slot // step].append(pltpu.make_async_copy(
            feats.at[table[slot]], x_all.at[:, pl.ds(slot * depth, depth)], x_sem.at[slot]))
    for part in range(2, parts):
        for n in range(3):
            copies[part].append(pltpu.make_async_copy(
                w_refs[part].at[:, n], w_all.at[n, pl.ds(part * step, step)], w_sem.at[n, part]))
    for part in copies:
        for copy in part:
            copy.start()
    out_copies = [
        pltpu.make_async_copy(
            w_refs[n].at[:, 3], w_out.at[pl.ds(n * step, step)], out_sem.at[n])
        for n in range(2, parts)
    ]
    chunk = mine.shape[0]
    out_copies.append(pltpu.make_async_copy(
        latents.at[pl.ds(pl.multiple_of(table[GROUP] * chunk, chunk), chunk)], mine, mine_sem))
    for copy in out_copies:
        copy.start()
    for n in range(2):
        w_out[pl.ds(n * step, step)] = w_refs[n][:, 3]
    sums = [None] * 3
    for part in range(parts):
        for copy in copies[part]:
            copy.wait()
        for n, top in enumerate((rows, 0, 0)):
            left = x_all[pl.ds(top, rows), pl.ds(part * step * depth, step * depth)]
            if part < 2:
                right = w_refs[part][:, n]
            else:
                right = w_all[n, pl.ds(part * step, step)]
            more = jnp.dot(left, right.reshape(step * depth, depth), preferred_element_type=F32)
            if part == 0:
                acc[n] = more
            elif part < parts - 1:
                acc[n] += more
            else:
                sums[n] = acc[n] + more
    query, keys, values = sums
    query = query.astype(BF16)
    keys = keys.astype(BF16)
    values = values.astype(BF16)
    scale = 1.0 / HEAD_DIM**0.5
    keep = valid[...] > 0
    lane = lax.broadcasted_iota(jnp.int32, (rows, HEAD_DIM), 1)
    tile = lax.broadcasted_iota(jnp.int32, (rows, HEAD_DIM), 0) // 8 % 4
    packed = jnp.zeros((rows, HEAD_DIM), F32)
    chunk = rows // GROUP
    for head in range(2):
        cols = slice(head * HEAD_DIM, (head + 1) * HEAD_DIM)
        scores = lax.dot_general(query[:, cols], keys[:, cols], (((1,), (1,)), ((), ())),
                                 preferred_element_type=F32) * scale
        scores = jnp.where(keep, scores, jnp.float32(-1000000000.0))
        top = jnp.max(scores, axis=1, keepdims=True)
        expo = jnp.exp(scores - top)
        total = jnp.sum(expo, axis=1, keepdims=True)
        coarse = expo.astype(BF16)
        fine = (expo - coarse.astype(F32)).astype(BF16)
        summed = jnp.dot(coarse, values[:, cols], preferred_element_type=F32)
        summed += jnp.dot(fine, values[:, cols], preferred_element_type=F32)
        out[:, pl.ds(head * chunk, chunk), :] = summed.reshape(GROUP, chunk, HEAD_DIM)
        packed = jnp.where(lane == 4 * tile + 2 * head, top, packed)
        packed = jnp.where(lane == 4 * tile + 2 * head + 1, total, packed)
    stat[...] = packed.reshape(GROUP, chunk // 8, 8, HEAD_DIM)
    out[:, pl.ds(2 * chunk, 8), :] = stat[:, 0] + stat[:, 1] + stat[:, 2] + stat[:, 3]
    for copy in out_copies:
        copy.wait()


def combine_kernel(parts, out):
    chunk = out.shape[1]
    stat = parts[:, pl.ds(2 * chunk, 8), :]
    factor = jnp.exp(stat - jnp.max(stat, axis=0, keepdims=True))
    lane = lax.broadcasted_iota(jnp.int32, (1, 8, HEAD_DIM), 2)
    factor = jnp.where(lane % 2 == 0, factor, 0.0)
    total = jnp.sum(pltpu.roll(factor, 1, 2) * stat, axis=0, keepdims=True)
    factor = factor / jnp.where(lane % 2 == 0, pltpu.roll(total, HEAD_DIM - 1, 2), 1.0)
    heads = []
    for head in range(2):
        tiles = []
        for tile in range(chunk // 8):
            at = 4 * tile + 2 * head
            rows = pl.ds(head * chunk + 8 * tile, 8)
            tiles.append(jnp.sum(parts[:, rows, :] * factor[:, :, at:at + 1], axis=0))
        heads.append(jnp.concatenate(tiles, axis=0))
    attended = jnp.concatenate(heads, axis=1).astype(BF16)
    for t in range(out.shape[0]):
        out[t] = attended


def project_kernel(table, mine, theirs, w_out, rows, upd, squares):
    chunk, depth = upd.shape
    core = table[GROUP + 1]
    lefts = []
    for slot in range(GROUP):
        block = table[slot]
        lefts.append(jnp.where(block % 2 == core, mine[block // 2], theirs[block // 2]))
    total = jnp.dot(jnp.concatenate(lefts, axis=1), w_out[...].reshape(GROUP * depth, depth),
                    preferred_element_type=F32)
    total += rows[...].astype(F32)
    upd[...] = total
    square = jnp.sum(total * total, axis=1, keepdims=True)
    lane = lax.broadcasted_iota(jnp.int32, (8, HEAD_DIM), 1)
    packed = jnp.zeros((8, HEAD_DIM), F32)
    for tile in range(chunk // 8):
        packed = jnp.where(lane == tile, square[8 * tile:8 * tile + 8], packed)
    for t in range(GROUP):
        squares[t] = packed


def finish_kernel(width, squares, upd, gain, out):
    total = jnp.sum(squares[...], axis=0)
    chunk, depth = upd.shape
    mean_sq = jnp.concatenate([total[:, n:n + 1] for n in range(chunk // 8)], axis=0) / width
    u = upd[...]
    normed = (gain[...] * u * lax.rsqrt(mean_sq + 1e-05)).astype(BF16)
    u = u.astype(BF16)
    for a in range(GROUP):
        out[a, :, pl.ds(0, depth)] = u
        out[a, :, pl.ds(depth, depth)] = normed


def whole(count):
    return [pl.BlockSpec(memory_space=pltpu.VMEM)] * count


def body(tokens, valid, latents, w_query, w_key, w_value, w_out, gain):
    rows, depth = tokens.shape
    chunk = latents.shape[0] // GROUP
    width = depth * lax.axis_size("tensor")
    both = jnp.concatenate([tokens, latents], axis=0)
    feats = lax.all_gather(both, "tensor", axis=0, tiled=False)
    weights = gather_weights(w_query, w_key, w_value, w_out)
    table = index_table()
    smem = pl.BlockSpec(memory_space=pltpu.SMEM)
    hbm = pl.BlockSpec(memory_space=pltpu.HBM)
    partial, out_weight, share = pl.pallas_call(
        attend_kernel,
        out_shape=(jax.ShapeDtypeStruct((GROUP, 2 * chunk + 8, HEAD_DIM), F32),
                   jax.ShapeDtypeStruct((GROUP, depth, depth), BF16),
                   jax.ShapeDtypeStruct((chunk, depth), BF16)),
        in_specs=[smem, hbm] + whole(2) + [hbm] * 6 + whole(1) + [hbm],
        out_specs=tuple(whole(3)),
        scratch_shapes=[
            pltpu.VMEM((2 * rows, GROUP * depth), BF16),
            pltpu.VMEM((3, GROUP, depth, depth), BF16),
            pltpu.VMEM((3, rows, depth), F32),
            pltpu.VMEM((GROUP, chunk // 8, 8, HEAD_DIM), F32),
            pltpu.SemaphoreType.DMA((GROUP,)),
            pltpu.SemaphoreType.DMA((3, 8)),
            pltpu.SemaphoreType.DMA((8,)),
            pltpu.SemaphoreType.DMA,
        ],
        compiler_params=pltpu.CompilerParams(vmem_limit_bytes=40 * 2**20),
        name="attend",
    )(table, feats, *weights, valid.reshape(1, rows), latents)
    partial = lax.all_to_all(partial, "agent", 0, 0)
    attended = pl.pallas_call(
        combine_kernel,
        out_shape=jax.ShapeDtypeStruct((GROUP // 2, chunk, depth), BF16),
        in_specs=whole(1),
        out_specs=whole(1)[0],
        compiler_params=pltpu.CompilerParams(vmem_limit_bytes=4 * 2**20),
        name="combine",
    )(partial)
    same_core = [list(range(core, GROUP, 2)) for core in range(2)]
    attended = lax.all_to_all(attended, "tensor", 0, 0, axis_index_groups=same_core)
    theirs = other_core(attended)
    upd, squares = pl.pallas_call(
        project_kernel,
        out_shape=(jax.ShapeDtypeStruct((chunk, depth), F32),
                   jax.ShapeDtypeStruct((GROUP, 8, HEAD_DIM), F32)),
        in_specs=[smem] + whole(4),
        out_specs=tuple(whole(2)),
        compiler_params=pltpu.CompilerParams(vmem_limit_bytes=8 * 2**20),
        name="project",
    )(table, attended, theirs, out_weight, share)
    squares = lax.all_to_all(squares, "tensor", 0, 0)
    out = pl.pallas_call(
        lambda *refs: finish_kernel(width, *refs),
        out_shape=jax.ShapeDtypeStruct((GROUP, chunk, 2 * depth), BF16),
        in_specs=whole(3),
        out_specs=whole(1)[0],
        compiler_params=pltpu.CompilerParams(vmem_limit_bytes=4 * 2**20),
        name="finish",
    )(squares, upd, gain.reshape(1, depth))
    out = lax.all_to_all(out, "agent", 0, 0)
    return out[:, :, :depth].reshape(-1, depth), out[:, :, depth:].reshape(-1, depth)


def solution(mesh):
    return jax.shard_map(
        body,
        mesh=mesh,
        in_specs=(
            P("agent", "tensor"),
            P("agent"),
            P(None, "tensor"),
            P("agent", "tensor"),
            P("agent", "tensor"),
            P("agent", "tensor"),
            P("agent", "tensor"),
            P("tensor"),
        ),
        out_specs=(P(None, "tensor"), P(None, "tensor")),
        check_vma=False,
    )
```
